128 devices in a mesh: seq: 32 (over z, x, core), dp: 4 (over y).
Axes of the slice: x: 4, y: 4, z: 4, core: 2. Of those that a mesh axis runs over, the one named last changes fastest.
Arguments:
- latents: bfloat16 [4, 64, 256, 1152], P('dp', 'seq'), may hold values from -24 to 24
- frame_counts: int32 [4], P('dp'), may hold values from 24 to 64, as said below
- mod_table: float32 [3, 1152], replicated, may hold values from -3 to 3
- clip_mod: float32 [4, 3, 1152], P('dp'), may hold values from -3 to 3
- q_gain: float32 [72], replicated, may hold values from 0.5 to 8
- k_gain: float32 [72], replicated, may hold values from 0.5 to 8
- w_qkv: bfloat16 [1152, 3456], replicated, may hold values from -0.1875 to 0.1875
- w_out: bfloat16 [1152, 1152], replicated, may hold values from -0.1875 to 0.1875
- cotangent: bfloat16 [4, 64, 256, 1152], P('dp', 'seq'), may hold values from -12 to 12
Outputs:
- block_out: bfloat16 [4, 64, 256, 1152], P('dp', 'seq')
- input_grad: bfloat16 [4, 64, 256, 1152], P('dp', 'seq')
- clip_mod_grad: float32 [4, 3, 1152], P('dp')
- table_grad: float32 [3, 1152], replicated
- q_gain_grad: float32 [72], replicated
- k_gain_grad: float32 [72], replicated
The draws below stay inside these ranges and needn't reach their ends.
Inputs may be any that keep to these rules, and one draw needn't show every extreme that they name: `frame_counts`: one clip of every draw fills all 64 frame slots.
All inputs are finite; a program needn't handle non-finite values.
Results may differ from the reference program's by a relative error of at most 0.02.
The reference program's roundings to bfloat16 on the way count: a program that leaves them out, or rounds other values in their place, can miss the bound.
Values may be sent and summed in bfloat16 or wider, within the bound.
No kernel may reach another device: no remote copies, remote signals or barrier semaphores. Data moves between devices by JAX's collectives and lax.ppermute only.
A program may use at most 192 MiB of HBM per device.

```python
import math
import jax
import jax.numpy as jnp
from jax import lax

HEAD_DIM = 72
D = 1152
P_DEV = 8
CLIPS = 4
FRAMES = 64
S_POS = 256


def draw_frame_counts(key, part):
    key = jax.random.fold_in(key, 1)
    first, second = jax.random.split(key)
    counts = jax.random.randint(first, (CLIPS,), 3 * FRAMES // 8, FRAMES + 1)
    fuller = jax.random.randint(second, (), 0, CLIPS)
    return jnp.where(jnp.arange(CLIPS, dtype=jnp.int32) == fuller, FRAMES, counts).astype(jnp.int32)


def draw_latents(key, part):
    key = jax.random.fold_in(key, 2)
    base_key, token_key, feature_key = jax.random.split(key, 3)
    shape = (CLIPS, FRAMES, S_POS, D)
    token_scale = jnp.exp(jax.random.uniform(token_key, (CLIPS, FRAMES, S_POS, 1), jnp.float32, math.log(0.3), math.log(3.0)))
    feature_scale = jnp.exp(jax.random.uniform(feature_key, (D,), jnp.float32, math.log(0.5), math.log(2.0)))
    base = jax.random.truncated_normal(base_key, -4.0, 4.0, shape, jnp.float32)
    return (base * token_scale * feature_scale).astype(jnp.bfloat16)


def draw_cotangent(key, part):
    key = jax.random.fold_in(key, 3)
    base_key = jax.random.fold_in(key, 0)
    shape = (CLIPS, FRAMES, S_POS, D)
    ramp = 1.0 + 2.0 * jnp.arange(FRAMES, dtype=jnp.float32) / (FRAMES - 1)
    ramp = ramp.reshape(1, FRAMES, 1, 1)
    base = jax.random.truncated_normal(base_key, -4.0, 4.0, shape, jnp.float32)
    return (base * ramp).astype(jnp.bfloat16)


def gain_values(key):
    return jax.random.uniform(key, (HEAD_DIM,), jnp.float32, 0.5, 1.5)


def draw_q_gain(key, part):
    key = jax.random.fold_in(key, 4)
    return gain_values(key)


def draw_k_gain(key, part):
    key = jax.random.fold_in(key, 5)
    return gain_values(key)


def level_of(key, extent, cuts, low, largest):
    def one(position, blocks):
        draws = jax.random.uniform(jax.random.fold_in(jax.random.fold_in(key, 6), position), (blocks,), jnp.float32, low / len(cuts), largest / len(cuts))
        return jnp.repeat(jnp.exp(draws), extent[position] // blocks).reshape((-1,) + (1,) * (len(extent) - position - 1))

    level = one(*cuts[0])
    for cut in cuts[1:]:
        level = level * one(*cut)
    return level


def noise(own_key, dims, deviation, bound, cuts=(), kind=jnp.bfloat16):
    drawn = deviation * jax.random.normal(own_key, dims, jnp.float32)
    if cuts:
        drawn = drawn * level_of(own_key, dims, cuts, -0.22, 0.18)
    return jnp.clip(drawn, -bound, bound).astype(kind)


def setup_inputs(seed: int = 0) -> dict:
    arg_keys = jax.random.split(jax.random.key(seed), 10)
    latents = draw_latents(jax.random.fold_in(arg_keys[9], 71), 0)
    frame_counts = draw_frame_counts(jax.random.fold_in(arg_keys[9], 71), 0)
    mod_table = noise(arg_keys[2], (3, D), 0.5, 3.0, (), jnp.float32)
    clip_mod = noise(arg_keys[3], (CLIPS, 3, D), 0.5, 3.0, ((0, 4),), jnp.float32)
    q_gain = draw_q_gain(jax.random.fold_in(arg_keys[9], 71), 0)
    k_gain = draw_k_gain(jax.random.fold_in(arg_keys[9], 71), 0)
    w_qkv = noise(arg_keys[6], (D, 3 * D), D ** -0.5, 0.1875)
    w_out = noise(arg_keys[7], (D, D), D ** -0.5, 0.1875)
    cotangent = draw_cotangent(jax.random.fold_in(arg_keys[9], 71), 0)
    return dict(latents=latents, frame_counts=frame_counts, mod_table=mod_table, clip_mod=clip_mod, q_gain=q_gain, k_gain=k_gain, w_qkv=w_qkv, w_out=w_out, cotangent=cotangent)


EPS = 1e-06

def layer_stats(flat_rows):
    row_mean = lax.optimization_barrier(jnp.mean(flat_rows, -1, keepdims=True))
    centred = flat_rows - row_mean
    inv_std = lax.rsqrt(lax.optimization_barrier(jnp.mean(centred * centred, -1, keepdims=True)) + EPS)
    return (centred * inv_std, inv_std)

def head_norm(projection, gain, heads):
    shaped = projection.reshape(projection.shape[0], heads, -1)
    inv_rms = lax.rsqrt(lax.optimization_barrier(jnp.mean(shaped * shaped, -1, keepdims=True)) + EPS)
    normal = (shaped * inv_rms * gain).astype(jnp.bfloat16)
    return (normal.reshape(projection.shape), inv_rms)

def head_norm_grad(projection, inv_rms, gain, grad_b16, heads):
    shaped = projection.reshape(projection.shape[0], heads, -1)
    upstream = grad_b16.astype(jnp.float32).reshape(shaped.shape)
    gain_part = lax.optimization_barrier(jnp.sum(upstream * shaped * inv_rms, axis=(0, 1)))
    scaled = upstream * gain
    inner = lax.optimization_barrier(jnp.mean(scaled * shaped, -1, keepdims=True))
    result = inv_rms * scaled - shaped * (inv_rms * inv_rms * inv_rms) * inner
    return (result.reshape(projection.shape), gain_part)

def attend_block(query, keys, vals, grad_out, key_valid, att_scale):
    query_f = query.astype(jnp.float32)
    keys_f = keys.astype(jnp.float32)
    vals_f = vals.astype(jnp.float32)
    grad_f = grad_out.astype(jnp.float32)
    scores = jnp.einsum('fphd,gphd->phfg', query_f, keys_f) * att_scale
    scores = jnp.where(key_valid, scores, jnp.float32(-1e+30))
    row_max = lax.optimization_barrier(jnp.max(scores, -1, keepdims=True))
    raised = jnp.exp(scores - row_max)
    prob_f32 = raised / lax.optimization_barrier(jnp.sum(raised, -1, keepdims=True))
    prob_b16 = lax.optimization_barrier(prob_f32.astype(jnp.bfloat16)).astype(jnp.float32)
    att_out = jnp.einsum('phfg,gphd->fphd', prob_b16, vals_f).astype(jnp.bfloat16)
    grad_prob = jnp.einsum('fphd,gphd->phfg', grad_f, vals_f)
    grad_vals = jnp.einsum('phfg,fphd->gphd', prob_b16, grad_f).astype(jnp.bfloat16)
    delta = lax.optimization_barrier(jnp.sum(prob_f32 * grad_prob, -1, keepdims=True))
    grad_score = prob_f32 * (grad_prob - delta) * att_scale
    grad_score = lax.optimization_barrier(grad_score.astype(jnp.bfloat16)).astype(jnp.float32)
    grad_query = jnp.einsum('phfg,gphd->fphd', grad_score, keys_f).astype(jnp.bfloat16)
    grad_keys = jnp.einsum('phfg,fphd->gphd', grad_score, query_f).astype(jnp.bfloat16)
    return (att_out, grad_query, grad_keys, grad_vals)

def one_clip(latent, clip_frames, modulation, grad_in, q_gain, k_gain, w_qkv, w_out):
    frames, positions, width = latent.shape
    heads = width // HEAD_DIM
    att_scale = HEAD_DIM ** (-0.5)
    mod_shift, mod_scale, mod_gate = (modulation[0], modulation[1], modulation[2])
    flat_rows = latent.reshape(-1, width).astype(jnp.float32)
    unit_rows, inv_std = layer_stats(flat_rows)
    normed = (unit_rows * (1.0 + mod_scale) + mod_shift).astype(jnp.bfloat16)
    projected = jnp.dot(normed, w_qkv, preferred_element_type=jnp.float32)
    q_proj = projected[:, :width]
    k_proj = projected[:, width:2 * width]
    v_proj = projected[:, 2 * width:]
    q_norm, q_inv = head_norm(q_proj, q_gain, heads)
    k_norm, k_inv = head_norm(k_proj, k_gain, heads)
    values = v_proj.astype(jnp.bfloat16)
    grad_rows = grad_in.reshape(-1, width).astype(jnp.float32)
    grad_y = (grad_rows * mod_gate).astype(jnp.bfloat16)
    grad_att = lax.dot_general(grad_y, w_out, (((1,), (1,)), ((), ())), preferred_element_type=jnp.float32).astype(jnp.bfloat16)
    blocks = positions // P_DEV

    def blockify(array):
        return array.reshape(frames, blocks, P_DEV, heads, HEAD_DIM).transpose(1, 0, 2, 3, 4)

    def unblock(array):
        return array.transpose(1, 0, 2, 3, 4).reshape(-1, width)
    key_valid = jnp.arange(frames, dtype=jnp.int32) < clip_frames

    def per_block(items):
        return attend_block(items[0], items[1], items[2], items[3], key_valid, att_scale)
    att_out, grad_qn, grad_kn, grad_vals = lax.map(per_block, (blockify(q_norm), blockify(k_norm), blockify(values), blockify(grad_att)))
    att_out = unblock(att_out)
    proj_y = jnp.dot(att_out, w_out, preferred_element_type=jnp.float32)
    block_out = (flat_rows + mod_gate * proj_y).astype(jnp.bfloat16)
    grad_q, q_part = head_norm_grad(q_proj, q_inv, q_gain, unblock(grad_qn), heads)
    grad_k, k_part = head_norm_grad(k_proj, k_inv, k_gain, unblock(grad_kn), heads)
    grad_qkv = jnp.concatenate([grad_q, grad_k, unblock(grad_vals).astype(jnp.float32)], 1).astype(jnp.bfloat16)
    grad_normed = lax.dot_general(grad_qkv, w_qkv, (((1,), (1,)), ((), ())), preferred_element_type=jnp.float32).astype(jnp.bfloat16)
    grad_h = lax.optimization_barrier(grad_normed).astype(jnp.float32)
    grad_shift = lax.optimization_barrier(jnp.sum(grad_h, 0))
    grad_scale = lax.optimization_barrier(jnp.sum(grad_h * unit_rows, 0))
    grad_gate = lax.optimization_barrier(jnp.sum(grad_rows * proj_y, 0))
    grad_unit = grad_h * (1.0 + mod_scale)
    grad_x = inv_std * (grad_unit - lax.optimization_barrier(jnp.mean(grad_unit, -1, keepdims=True)) - unit_rows * lax.optimization_barrier(jnp.mean(grad_unit * unit_rows, -1, keepdims=True)))
    input_grad = (grad_rows + grad_x).astype(jnp.bfloat16)
    mod_grad = jnp.stack([grad_shift, grad_scale, grad_gate])
    return (block_out.reshape(latent.shape), input_grad.reshape(latent.shape), mod_grad, q_part, k_part)

def reference(latents, frame_counts, mod_table, clip_mod, q_gain, k_gain, w_qkv, w_out, cotangent):
    modulations = mod_table[None] + clip_mod

    def per_clip(items):
        return one_clip(items[0], items[1], items[2], items[3], q_gain, k_gain, w_qkv, w_out)
    block_out, input_grad, mod_grad, q_parts, k_parts = lax.map(per_clip, (latents, frame_counts, modulations, cotangent))
    return (block_out, input_grad, mod_grad, lax.optimization_barrier(jnp.sum(mod_grad, 0)), lax.optimization_barrier(jnp.sum(q_parts, 0)), lax.optimization_barrier(jnp.sum(k_parts, 0)))
```

```python
import jax
import jax.numpy as jnp
from jax import lax
from jax.experimental import pallas as pl
from jax.experimental.pallas import tpu as pltpu
from jax.sharding import PartitionSpec as P

EPS = 1e-06
F32 = jnp.float32
BF16 = jnp.bfloat16
HEAD = 72
HEADS = 16
D = HEAD * HEADS
MAIN = 64 * HEADS
REST = 8 * HEADS
TOK = 512
POS = 8
FR = 64
ROWS = 128
PAIRS = TOK // ROWS
VMEM = 56 * 1024 * 1024
NN = (((1,), (0,)), ((), ()))
NT = (((1,), (1,)), ((), ()))
TN = (((0,), (0,)), ((), ()))


def dot(a, b, dims=NN):
    return lax.dot_general(a, b, dims, preferred_element_type=F32)


def iota(shape, dim):
    return lax.broadcasted_iota(jnp.int32, shape, dim)


def one_hot(cond):
    return jnp.where(cond, jnp.float32(1), jnp.float32(0)).astype(BF16)


def source_main(col):
    return col + 8 * (col >> 6)


def source_rest(col):
    return col + 64 + 64 * (col >> 3)


def split_columns(w_ref, o_ref):
    for part in range(3):
        base = part * D
        for j in range(4):
            lo = (288 * j) // 128 * 128
            r, c = iota((384, 256), 0), iota((384, 256), 1)
            pick = one_hot(source_main(c + 256 * j) == r + lo)
            o_ref[:, part * MAIN + 256 * j : part * MAIN + 256 * (j + 1)] = dot(
                w_ref[:, base + lo : base + lo + 384], pick
            ).astype(BF16)
        r, c = iota((D, REST), 0), iota((D, REST), 1)
        pick = one_hot(source_rest(c) == r)
        o_ref[:, 3 * MAIN + part * REST : 3 * MAIN + (part + 1) * REST] = dot(
            w_ref[:, base : base + D], pick
        ).astype(BF16)


def split_rows(w_ref, o_ref):
    for j in range(4):
        lo = (288 * j) // 128 * 128
        r, c = iota((256, 384), 0), iota((256, 384), 1)
        pick = one_hot(source_main(r + 256 * j) == c + lo)
        o_ref[256 * j : 256 * (j + 1), :] = dot(pick, w_ref[lo : lo + 384, :]).astype(BF16)
    r, c = iota((REST, D), 0), iota((REST, D), 1)
    pick = one_hot(source_rest(r) == c)
    o_ref[MAIN:, :] = dot(pick, w_ref[...]).astype(BF16)


def split_weights(w_qkv, w_out):
    steps = 4
    rows = D // steps
    wq = pl.pallas_call(
        split_columns,
        grid=(steps,),
        in_specs=[pl.BlockSpec((rows, 3 * D), lambda i: (i, 0))],
        out_specs=pl.BlockSpec((rows, 3 * D), lambda i: (i, 0)),
        out_shape=jax.ShapeDtypeStruct((D, 3 * D), BF16),
        compiler_params=pltpu.CompilerParams(vmem_limit_bytes=VMEM),
        cost_estimate=pl.CostEstimate(
            flops=2 * D * D * 1200, bytes_accessed=12 * D * D, transcendentals=0
        ),
        name="split_columns",
    )(w_qkv)
    cols = D // 3
    wo = pl.pallas_call(
        split_rows,
        grid=(3,),
        in_specs=[pl.BlockSpec((D, cols), lambda i: (0, i))],
        out_specs=pl.BlockSpec((D, cols), lambda i: (0, i)),
        out_shape=jax.ShapeDtypeStruct((D, D), BF16),
        compiler_params=pltpu.CompilerParams(vmem_limit_bytes=VMEM),
        cost_estimate=pl.CostEstimate(
            flops=2 * D * D * 400, bytes_accessed=4 * D * D, transcendentals=0
        ),
        name="split_rows",
    )(w_out)
    return wq, wo


def to_positions(start):
    r, c = iota((ROWS, TOK), 0) + start, iota((ROWS, TOK), 1)
    return one_hot(c == (r & (FR - 1)) * POS + (r >> 6))


def to_frames(start):
    r, c = iota((ROWS, TOK), 0) + start, iota((ROWS, TOK), 1)
    return one_hot(c == (r & (POS - 1)) * FR + (r >> 3))


def halves(value):
    high = value.astype(BF16)
    return high, (value - high.astype(F32)).astype(BF16)


def init_segments(seg, spread):
    r, c = iota((D, REST), 0), iota((D, REST), 1)
    head = jnp.where(r < MAIN, r >> 6, (r - MAIN) >> 3)
    seg[...] = one_hot(head == (c >> 3))
    r, c = iota((2 * REST, MAIN), 0), iota((2 * REST, MAIN), 1)
    spread[...] = one_hot((r & (REST - 1)) == 8 * (c >> 6))


def head_sums(main, rest, seg):
    mh, ml = halves(main)
    rh, rl = halves(rest)
    return (
        dot(mh, seg[:MAIN, :]) + dot(ml, seg[:MAIN, :]) + dot(rh, seg[MAIN:, :]) + dot(rl, seg[MAIN:, :])
    )


def expand(per_head, spread):
    high, low = halves(per_head)
    return dot(jnp.concatenate([high, low], 1), spread[...])


def head_masks(t):
    c = iota((1, 256), 1)
    head = jnp.where(c < 128, (c >> 6) + 2 * t, (c - 128) >> 3)
    out = [one_hot(head == h) for h in (2 * t, 2 * t + 1)]
    return out


def stacked(block, masks):
    return jnp.concatenate([block * masks[0], block * masks[1]], 0)


def unit_of(ref, rows, t):
    return jnp.concatenate([ref[rows, 128 * t : 128 * (t + 1)], ref[rows, MAIN:]], 1)


def rows_of(i):
    return pl.ds(pl.multiple_of(i * ROWS, ROWS), ROWS)


def over_columns(total, body):
    def step(b, _):
        body(pl.ds(pl.multiple_of(b * 256, 256), 256))
        return 0

    lax.fori_loop(0, total // 256, step, 0)
    if total % 256:
        body(pl.ds(total // 256 * 256, total % 256))


def over_pairs(body):
    def step(i, _):
        body(i)
        return 0

    lax.fori_loop(0, PAIRS, step, 0)


def forward(
    count_ref,
    x_ref,
    mod_ref,
    gain_ref,
    wqkv_ref,
    wout_ref,
    bo_ref,
    unit_ref,
    istd_ref,
    qhat_ref,
    khat_ref,
    rq_ref,
    rk_ref,
    qn_ref,
    kn_ref,
    vn_ref,
    prob_ref,
    y_ref,
    xp,
    normed,
    proj,
    att,
    bo,
    seg,
    spread,
    bias,
):
    init_segments(seg, spread)
    r, c = iota((256, 128), 0), iota((256, 128), 1)
    valid = (((r >> 6) & 1) == (c >> 6)) & ((r & (FR - 1)) < count_ref[0])
    bias[...] = jnp.where(valid, jnp.float32(0), jnp.float32(-1e30))

    def norm(i):
        rows = rows_of(i)
        x = dot(to_positions(i * ROWS), x_ref[...])
        xp[rows, :] = x
        centred = x - jnp.mean(x, -1, keepdims=True)
        inv = lax.rsqrt(jnp.mean(centred * centred, -1, keepdims=True) + EPS)
        unit = centred * inv
        unit_ref[rows, :] = unit
        istd_ref[rows, :] = jnp.broadcast_to(inv, (ROWS, 128))
        normed[rows, :] = (unit * (1.0 + mod_ref[1:2, :]) + mod_ref[0:1, :]).astype(BF16)

    over_pairs(norm)

    def project(cols):
        proj[:, cols] = dot(normed[...], wqkv_ref[:, cols])

    over_columns(3 * D, project)

    def heads(i):
        rows = rows_of(i)
        for part, (n_ref, hat_ref, r_ref) in enumerate(
            ((qn_ref, qhat_ref, rq_ref), (kn_ref, khat_ref, rk_ref))
        ):
            main = proj[rows, part * MAIN : (part + 1) * MAIN]
            rest = proj[rows, 3 * MAIN + part * REST : 3 * MAIN + (part + 1) * REST]
            inv = lax.rsqrt(head_sums(main * main, rest * rest, seg) * (1.0 / HEAD) + EPS)
            r_ref[rows, :] = inv
            main = main * expand(inv, spread)
            rest = rest * inv
            hat_ref[rows, :MAIN] = main
            hat_ref[rows, MAIN:] = rest
            gain = gain_ref[part : part + 1, :]
            n_ref[rows, :MAIN] = (main * gain[:, :MAIN]).astype(BF16)
            n_ref[rows, MAIN:] = (rest * gain[:, MAIN:]).astype(BF16)
        vn_ref[rows, :MAIN] = proj[rows, 2 * MAIN : 3 * MAIN].astype(BF16)
        vn_ref[rows, MAIN:] = proj[rows, 3 * MAIN + 2 * REST :].astype(BF16)

    over_pairs(heads)

    def attend(i):
        rows = rows_of(i)
        total = jnp.zeros((ROWS, REST), F32)
        for t in range(HEADS // 2):
            masks = head_masks(t)
            keys = stacked(unit_of(kn_ref, rows, t), masks)
            s = dot(keys, unit_of(qn_ref, rows, t), NT) * (HEAD**-0.5) + bias[...]
            s = s.reshape(2, 128, 128)
            e = jnp.exp(s - jnp.max(s, 1, keepdims=True))
            prob = (e / jnp.sum(e, 1, keepdims=True)).reshape(256, 128)
            prob_ref[i, t] = prob
            out = dot(prob.astype(BF16), stacked(unit_of(vn_ref, rows, t), masks), TN)
            att[rows, 128 * t : 128 * (t + 1)] = out[:, :128].astype(BF16)
            total = total + out[:, 128:]
        att[rows, MAIN:] = total.astype(BF16)

    over_pairs(attend)

    def out_project(cols):
        y = dot(att[...], wout_ref[:, cols])
        y_ref[:, cols] = y
        bo[:, cols] = (xp[:, cols] + mod_ref[2:3, cols] * y).astype(BF16)

    over_columns(D, out_project)

    def emit(i):
        bo_ref[rows_of(i), :] = dot(to_frames(i * ROWS), bo[...]).astype(BF16)

    over_pairs(emit)


def backward(
    cot_ref,
    mod_ref,
    gain_ref,
    wqkv_ref,
    wout_ref,
    bo_ref,
    unit_ref,
    istd_ref,
    qhat_ref,
    khat_ref,
    rq_ref,
    rk_ref,
    qn_ref,
    kn_ref,
    vn_ref,
    prob_ref,
    y_ref,
    out_ref,
    sum_ref,
    cp,
    gy,
    gatt,
    dq,
    dk,
    dqkv,
    gn,
    ig,
    seg,
    spread,
):
    ranks = TOK // 16
    init_segments(seg, spread)
    out_ref[:, :16, :] = bo_ref[...].reshape(ranks, 16, D)
    sum_ref[...] = jnp.zeros_like(sum_ref)

    def arrive(i):
        rows = rows_of(i)
        cot = dot(to_positions(i * ROWS), cot_ref[...])
        cp[rows, :] = cot
        gy[rows, :] = (cot * mod_ref[2:3, :]).astype(BF16)
        sum_ref[2:3, :] += jnp.sum(cot * y_ref[rows, :], 0, keepdims=True)

    over_pairs(arrive)

    def grad_attention(rows256):
        gatt[:, rows256] = dot(gy[...], wout_ref[rows256, :], NT).astype(BF16)

    over_columns(D, grad_attention)

    def attend(i):
        rows = rows_of(i)
        rest_q = jnp.zeros((ROWS, REST), F32)
        rest_k = jnp.zeros((ROWS, REST), F32)
        rest_v = jnp.zeros((ROWS, REST), F32)
        for t in range(HEADS // 2):
            masks = head_masks(t)
            cols = slice(128 * t, 128 * (t + 1))
            grad = unit_of(gatt, rows, t)
            prob = prob_ref[i, t]
            dp = dot(stacked(unit_of(vn_ref, rows, t), masks), grad, NT)
            w = (prob * dp).reshape(2, 128, 128)
            delta = jnp.broadcast_to(jnp.sum(w, 1, keepdims=True), (2, 128, 128)).reshape(256, 128)
            ds = (prob * (dp - delta) * (HEAD**-0.5)).astype(BF16)
            pb = prob.astype(BF16)
            g = dot(ds, stacked(unit_of(kn_ref, rows, t), masks), TN)
            dq[rows, cols] = g[:, :128].astype(BF16)
            rest_q = rest_q + g[:, 128:]
            side = jnp.concatenate([ds[:128], ds[128:]], 1)
            g = dot(side, stacked(unit_of(qn_ref, rows, t), masks))
            dk[rows, cols] = g[:, :128].astype(BF16)
            rest_k = rest_k + g[:, 128:]
            side = jnp.concatenate([pb[:128], pb[128:]], 1)
            g = dot(side, stacked(grad, masks))
            dqkv[rows, 2 * MAIN + 128 * t : 2 * MAIN + 128 * (t + 1)] = g[:, :128].astype(BF16)
            rest_v = rest_v + g[:, 128:]
        dq[rows, MAIN:] = rest_q.astype(BF16)
        dk[rows, MAIN:] = rest_k.astype(BF16)
        dqkv[rows, 3 * MAIN + 2 * REST :] = rest_v.astype(BF16)

    over_pairs(attend)

    def heads(i):
        rows = rows_of(i)
        for part, (d_ref, hat_ref, r_ref) in enumerate(
            ((dq, qhat_ref, rq_ref), (dk, khat_ref, rk_ref))
        ):
            gain = gain_ref[part : part + 1, :]
            up = d_ref[rows, :].astype(F32)
            hat = hat_ref[rows, :]
            sum_ref[3 + part : 4 + part, :] += jnp.sum(up * hat, 0, keepdims=True)
            a = up * gain
            w = a * hat
            inner = head_sums(w[:, :MAIN], w[:, MAIN:], seg) * (1.0 / HEAD)
            inv = r_ref[rows, :]
            main = expand(inv, spread) * (a[:, :MAIN] - hat[:, :MAIN] * expand(inner, spread))
            rest = inv * (a[:, MAIN:] - hat[:, MAIN:] * inner)
            dqkv[rows, part * MAIN : (part + 1) * MAIN] = main.astype(BF16)
            dqkv[rows, 3 * MAIN + part * REST : 3 * MAIN + (part + 1) * REST] = rest.astype(BF16)

    over_pairs(heads)

    def grad_normed(rows256):
        gn[:, rows256] = dot(dqkv[...], wqkv_ref[rows256, :], NT).astype(BF16)

    over_columns(D, grad_normed)

    def layer(i):
        rows = rows_of(i)
        g = gn[rows, :].astype(F32)
        unit = unit_ref[rows, :]
        sum_ref[0:1, :] += jnp.sum(g, 0, keepdims=True)
        sum_ref[1:2, :] += jnp.sum(g * unit, 0, keepdims=True)
        u = g * (1.0 + mod_ref[1:2, :])
        first = jnp.mean(u, -1, keepdims=True)
        second = jnp.mean(u * unit, -1, keepdims=True)
        grad_x = istd_ref[rows, 0:1] * (u - first - unit * second)
        ig[rows, :] = (cp[rows, :] + grad_x).astype(BF16)

    over_pairs(layer)

    def emit(i):
        value = dot(to_frames(i * ROWS), ig[...]).astype(BF16)
        out_ref[pl.ds(i * 8, 8), 16:, :] = value.reshape(8, 16, D)

    over_pairs(emit)


def vmem_call(kernel, outs, scratch, flops, name, n_in, scalars=0):
    return pl.pallas_call(
        kernel,
        in_specs=[pl.BlockSpec(memory_space=pltpu.SMEM)] * scalars
        + [pl.BlockSpec(memory_space=pltpu.VMEM)] * (n_in - scalars),
        out_specs=[pl.BlockSpec(memory_space=pltpu.VMEM)] * len(outs),
        out_shape=[jax.ShapeDtypeStruct(s, d) for s, d in outs],
        scratch_shapes=[pltpu.VMEM(s, d) for s, d in scratch],
        compiler_params=pltpu.CompilerParams(vmem_limit_bytes=VMEM),
        cost_estimate=pl.CostEstimate(flops=flops, bytes_accessed=30_000_000, transcendentals=0),
        name=name,
    )


def sum_over(value, axis, size):
    step = 1
    while step < size:
        value = value + lax.ppermute(value, axis, [(i, i ^ step) for i in range(size)])
        step *= 2
    return value


def split_gain(gain):
    return jnp.concatenate([jnp.tile(gain[:64], HEADS), jnp.tile(gain[64:], HEADS)])


def join_gain(row):
    return jnp.concatenate(
        [row[:MAIN].reshape(HEADS, 64).sum(0), row[MAIN:].reshape(HEADS, 8).sum(0)]
    )


def shards(latents, frame_counts, mod_table, clip_mod, q_gain, k_gain, w_qkv, w_out, cotangent):
    ranks = lax.axis_size("seq")
    modulation = mod_table + clip_mod[0]
    gains = jnp.stack([split_gain(q_gain), split_gain(k_gain)])

    def exchange(rows):
        return lax.all_to_all(rows, "seq", split_axis=0, concat_axis=0, tiled=True)

    def outgoing(array):
        return array.reshape(2, ranks, POS, D).transpose(1, 0, 2, 3).reshape(ranks, 16, D)

    def incoming(array):
        return array.reshape(ranks, 2, POS, D).transpose(1, 0, 2, 3).reshape(latents.shape)

    x = exchange(outgoing(latents)).reshape(TOK, D)
    cot = exchange(outgoing(cotangent)).reshape(TOK, D)
    wqkv, wout = split_weights(w_qkv, w_out)
    tok = (TOK, D)
    saved = [
        (tok, BF16),
        (tok, F32),
        ((TOK, 128), F32),
        (tok, F32),
        (tok, F32),
        ((TOK, REST), F32),
        ((TOK, REST), F32),
        (tok, BF16),
        (tok, BF16),
        (tok, BF16),
        ((PAIRS, HEADS // 2, 256, 128), F32),
        (tok, F32),
    ]
    helpers = [((D, REST), BF16), ((2 * REST, MAIN), BF16)]
    residuals = vmem_call(
        forward,
        saved,
        [(tok, F32), (tok, BF16), ((TOK, 3 * D), F32), (tok, BF16), (tok, BF16)]
        + helpers
        + [((256, 128), F32)],
        8_000_000_000,
        "attention_forward",
        6,
        1,
    )(frame_counts, x, modulation, gains, wqkv, wout)
    out, sums = vmem_call(
        backward,
        [((ranks, 32, D), BF16), ((8, D), F32)],
        [(tok, F32)] + [(tok, BF16)] * 4 + [((TOK, 3 * D), BF16)] + [(tok, BF16)] * 2 + helpers,
        9_000_000_000,
        "attention_backward",
        5 + len(saved),
    )(cot, modulation, gains, wqkv, wout, *residuals)
    back = exchange(out)
    block_out = incoming(back[:, :16, :])
    input_grad = incoming(back[:, 16:, :])
    clip_total = sum_over(sums, "seq", ranks)
    table_total = sum_over(clip_total, "dp", lax.axis_size("dp"))
    return (
        block_out,
        input_grad,
        clip_total[None, :3],
        table_total[:3],
        join_gain(table_total[3]),
        join_gain(table_total[4]),
    )


def solution(mesh):
    return jax.shard_map(
        shards,
        mesh=mesh,
        in_specs=(
            P("dp", "seq", None, None),
            P("dp"),
            P(),
            P("dp", None, None),
            P(),
            P(),
            P(),
            P(),
            P("dp", "seq", None, None),
        ),
        out_specs=(
            P("dp", "seq", None, None),
            P("dp", "seq", None, None),
            P("dp", None, None),
            P(),
            P(),
            P(),
        ),
        check_vma=False,
    )
```

```python
import jax
import jax.numpy as jnp
from jax import lax
from jax.experimental import pallas as pl
from jax.experimental.pallas import tpu as pltpu
from jax.sharding import PartitionSpec as P

EPS = 1e-06
F32 = jnp.float32
BF16 = jnp.bfloat16
HEAD = 72
HEADS = 16
D = HEAD * HEADS
MAIN = 64 * HEADS
REST = 8 * HEADS
QK = 2 * D
MAIN_AT = (0, MAIN, QK)
REST_AT = (2 * MAIN, 2 * MAIN + REST, QK + MAIN)
TOK = 512
POS = 8
FR = 64
ROWS = 128
PAIRS = TOK // ROWS
BLOCK = 512
LANES = 128
TILES = D // LANES
SUMS = 16
SENT = 32 + SUMS
VMEM = 56 * 1024 * 1024
NN = (((1,), (0,)), ((), ()))
NT = (((1,), (1,)), ((), ()))
TN = (((0,), (0,)), ((), ()))


def dot(a, b, dims=NN):
    return lax.dot_general(a, b, dims, preferred_element_type=F32)


def iota(shape, dim):
    return lax.broadcasted_iota(jnp.int32, shape, dim)


def one_hot(cond):
    return jnp.where(cond, jnp.float32(1), jnp.float32(0)).astype(BF16)


def source_main(col):
    return col + 8 * (col >> 6)


def source_rest(col):
    return col + 64 + 64 * (col >> 3)


def split_columns(w_ref, o_ref):
    for part in range(3):
        base = part * D
        for j in range(4):
            lo = (288 * j) // 128 * 128
            r, c = iota((384, 256), 0), iota((384, 256), 1)
            pick = one_hot(source_main(c + 256 * j) == r + lo)
            o_ref[:, MAIN_AT[part] + 256 * j : MAIN_AT[part] + 256 * (j + 1)] = dot(
                w_ref[:, base + lo : base + lo + 384], pick
            ).astype(BF16)
        r, c = iota((D, REST), 0), iota((D, REST), 1)
        pick = one_hot(source_rest(c) == r)
        o_ref[:, REST_AT[part] : REST_AT[part] + REST] = dot(
            w_ref[:, base : base + D], pick
        ).astype(BF16)


def split_rows(w_ref, o_ref):
    for j in range(4):
        lo = (288 * j) // 128 * 128
        r, c = iota((256, 384), 0), iota((256, 384), 1)
        pick = one_hot(source_main(r + 256 * j) == c + lo)
        o_ref[256 * j : 256 * (j + 1), :] = dot(pick, w_ref[lo : lo + 384, :]).astype(BF16)
    r, c = iota((REST, D), 0), iota((REST, D), 1)
    pick = one_hot(source_rest(r) == c)
    o_ref[MAIN:, :] = dot(pick, w_ref[...]).astype(BF16)


def split_weights(w_qkv, w_out):
    steps = 4
    rows = D // steps
    wq = pl.pallas_call(
        split_columns,
        grid=(steps,),
        in_specs=[pl.BlockSpec((rows, 3 * D), lambda i: (i, 0))],
        out_specs=pl.BlockSpec((rows, 3 * D), lambda i: (i, 0)),
        out_shape=jax.ShapeDtypeStruct((D, 3 * D), BF16),
        compiler_params=pltpu.CompilerParams(vmem_limit_bytes=VMEM),
        cost_estimate=pl.CostEstimate(
            flops=2 * D * D * 1200, bytes_accessed=12 * D * D, transcendentals=0
        ),
        name="split_columns",
    )(w_qkv)
    cols = D // 3
    wo = pl.pallas_call(
        split_rows,
        grid=(3,),
        in_specs=[pl.BlockSpec((D, cols), lambda i: (0, i))],
        out_specs=pl.BlockSpec((D, cols), lambda i: (0, i)),
        out_shape=jax.ShapeDtypeStruct((D, D), BF16),
        compiler_params=pltpu.CompilerParams(vmem_limit_bytes=VMEM),
        cost_estimate=pl.CostEstimate(
            flops=2 * D * D * 400, bytes_accessed=4 * D * D, transcendentals=0
        ),
        name="split_rows",
    )(w_out)
    return wq, wo


def init_segments(seg, spread, fold):
    r, c = iota((D, REST), 0), iota((D, REST), 1)
    head = jnp.where(r < MAIN, r >> 6, (r - MAIN) >> 3)
    seg[...] = one_hot(head == (c >> 3))
    entry = jnp.where(r < MAIN, r & 63, 64 + (r & 7))
    fold[...] = one_hot(entry == c)
    r, c = iota((2 * REST, MAIN), 0), iota((2 * REST, MAIN), 1)
    spread[...] = one_hot((r & (REST - 1)) == 8 * (c >> 6))


def terms(value):
    high = value.astype(BF16)
    left = value - high.astype(F32)
    mid = left.astype(BF16)
    return high, mid, (left - mid.astype(F32)).astype(BF16)


def both(per_head):
    high = per_head.astype(BF16)
    return jnp.concatenate([high, (per_head - high.astype(F32)).astype(BF16)], 1)


def head_masks(t):
    c = iota((1, 256), 1)
    head = jnp.where(c < 128, (c >> 6) + 2 * t, (c - 128) >> 3)
    return [one_hot(head == h) for h in (2 * t, 2 * t + 1)]


def unit_of(ref, rows, t):
    return jnp.concatenate([ref[rows, 128 * t : 128 * (t + 1)], ref[rows, MAIN:]], 1)


def stacked(block, masks):
    return [
        jnp.concatenate([block[:FR] * masks[0], block[:FR] * masks[1]], 0),
        jnp.concatenate([block[FR:] * masks[0], block[FR:] * masks[1]], 0),
    ]


def diagonal(block):
    zero = jnp.zeros((FR, 256), BF16)
    return jnp.concatenate(
        [
            jnp.concatenate([block[:FR], zero], 1),
            jnp.concatenate([zero, block[FR:]], 1),
        ],
        0,
    )


def own_features(product, masks):
    zero, one = masks[0].astype(F32), masks[1].astype(F32)
    return jnp.concatenate(
        [
            product[:FR, :256] * zero + product[FR:, :256] * one,
            product[:FR, 256:] * zero + product[FR:, 256:] * one,
        ],
        0,
    )


def loop(count, body):
    def step(i, _):
        body(i)
        return 0

    lax.fori_loop(0, count, step, 0)


def over_columns(total, body):
    loop(total // BLOCK, lambda b: body(pl.ds(pl.multiple_of(b * BLOCK, BLOCK), BLOCK)))
    if total % BLOCK:
        body(pl.ds(total // BLOCK * BLOCK, total % BLOCK))


def over_rows(size, body):
    loop(TOK // size, lambda i: body(pl.ds(pl.multiple_of(i * size, size), size)))


def lane_tiles():
    return [slice(LANES * c, LANES * (c + 1)) for c in range(TILES)]


def sub_block(
    count_ref,
    in_ref,
    mod_ref,
    gain_ref,
    wqkv_hbm,
    wout_hbm,
    out_ref,
    wqkv,
    wout,
    sems,
    frames,
    xp,
    unit,
    istd,
    cp,
    gy,
    normed,
    proj,
    gatt,
    qn,
    kn,
    vn,
    rq,
    rk,
    dq,
    dk,
    dqkv,
    sums,
    seg,
    spread,
    fold,
    bias,
):
    ranks = in_ref.shape[0]
    att, gn = gy, normed
    load_qkv = pltpu.make_async_copy(wqkv_hbm, wqkv, sems.at[0])
    load_out = pltpu.make_async_copy(wout_hbm, wout, sems.at[1])
    load_out.start()
    load_qkv.start()
    init_segments(seg, spread, fold)
    r = iota((128, 128), 0)
    bias[...] = jnp.where((r & (FR - 1)) < count_ref[0], jnp.float32(0), jnp.float32(-1e30))
    sums[...] = jnp.zeros_like(sums)

    def at_position(p):
        return pl.ds(p, FR, stride=POS)

    def position_rows(p):
        return pl.ds(pl.multiple_of(p * FR, FR), FR)

    def fill(first):
        for c, cols in enumerate(lane_tiles()):
            frames[c] = in_ref[:, first : first + 16, cols].reshape(TOK, LANES).astype(F32)

    def drain(first):
        for c, cols in enumerate(lane_tiles()):
            out_ref[:, first : first + 16, cols] = frames[c].astype(BF16).reshape(ranks, 16, LANES)

    def arrive(p):
        rows = position_rows(p)
        for c, cols in enumerate(lane_tiles()):
            cot = frames[c, at_position(p), :]
            cp[rows, cols] = cot
            gy[rows, cols] = (cot * mod_ref[2:3, cols]).astype(BF16)

    def norm(p):
        rows = position_rows(p)
        parts = [frames[c, at_position(p), :] for c in range(TILES)]
        mean = jnp.sum(sum(parts), -1, keepdims=True) * (1.0 / D)
        centred = [x - mean for x in parts]
        square = jnp.sum(sum(x * x for x in centred), -1, keepdims=True) * (1.0 / D)
        inv = lax.rsqrt(square + EPS)
        istd[rows, :] = jnp.broadcast_to(inv, (FR, LANES))
        for c, cols in enumerate(lane_tiles()):
            xp[rows, cols] = parts[c]
            u = centred[c] * inv
            unit[rows, cols] = u
            normed[rows, cols] = (u * (1.0 + mod_ref[1:2, cols]) + mod_ref[0:1, cols]).astype(BF16)

    fill(16)
    loop(POS, arrive)
    fill(0)
    loop(POS, norm)

    def grad_attention(cols):
        gatt[:, cols] = dot(gy[...], wout[cols, :], NT).astype(BF16)

    load_out.wait()
    over_columns(D, grad_attention)

    def project(cols):
        proj[:, cols] = dot(normed[...], wqkv[:, cols])

    load_qkv.wait()
    over_columns(QK, project)

    def project_values(cols):
        vn[:, cols] = dot(normed[...], wqkv[:, pl.ds(QK + cols.start, cols.size)]).astype(BF16)

    over_columns(D, project_values)

    def heads(rows):
        for part, (n_ref, r_ref) in enumerate(((qn, rq), (kn, rk))):
            main = slice(MAIN_AT[part], MAIN_AT[part] + MAIN)
            rest = slice(REST_AT[part], REST_AT[part] + REST)
            m, t = proj[rows, main], proj[rows, rest]
            total = sum(dot(part, seg[:MAIN, :]) for part in terms(m * m)[:2])
            total = total + sum(dot(part, seg[MAIN:, :]) for part in terms(t * t)[:2])
            inv = lax.rsqrt(total * (1.0 / HEAD) + EPS)
            r_ref[rows, :] = inv
            pair = both(inv)
            for b in range(0, MAIN, 256):
                cols = slice(MAIN_AT[part] + b, MAIN_AT[part] + b + 256)
                hat = proj[rows, cols] * dot(pair, spread[:, b : b + 256])
                proj[rows, cols] = hat
                n_ref[rows, b : b + 256] = (hat * gain_ref[part : part + 1, b : b + 256]).astype(BF16)
            hat = t * inv
            proj[rows, rest] = hat
            n_ref[rows, MAIN:] = (hat * gain_ref[part : part + 1, MAIN:]).astype(BF16)

    over_rows(256, heads)

    def attend(rows):
        rest = [jnp.zeros((ROWS, REST), F32)] * 4
        for t in range(HEADS // 2):
            masks = head_masks(t)
            cols = slice(128 * t, 128 * (t + 1))
            keys = stacked(unit_of(kn, rows, t), masks)
            vals = stacked(unit_of(vn, rows, t), masks)
            query = diagonal(unit_of(qn, rows, t))
            grad = diagonal(unit_of(gatt, rows, t))
            s = dot(jnp.concatenate(keys, 1), query, NT) * (HEAD**-0.5) + bias[...]
            s = s.reshape(2, FR, 128)
            e = jnp.exp(s - jnp.max(s, 1, keepdims=True))
            prob = e * (1.0 / jnp.sum(e, 1, keepdims=True))
            dp = dot(jnp.concatenate(vals, 1), grad, NT).reshape(2, FR, 128)
            delta = jnp.sum(prob * dp, 1, keepdims=True)
            ds = (prob * (dp - delta) * (HEAD**-0.5)).reshape(128, 128)
            prob = prob.reshape(128, 128)
            pb, db = prob.astype(BF16), ds.astype(BF16)
            pt, dt = prob.T.astype(BF16), ds.T.astype(BF16)
            out = jnp.concatenate([dot(pt[:FR], vals[0]), dot(pt[FR:], vals[1])], 0)
            gq = jnp.concatenate([dot(dt[:FR], keys[0]), dot(dt[FR:], keys[1])], 0)
            gk = own_features(dot(db, query), masks)
            gv = own_features(dot(pb, grad), masks)
            att[rows, cols] = out[:, :128].astype(BF16)
            dq[rows, cols] = gq[:, :128].astype(BF16)
            dk[rows, cols] = gk[:, :128].astype(BF16)
            dqkv[rows, QK + 128 * t : QK + 128 * (t + 1)] = gv[:, :128].astype(BF16)
            rest = [a + b[:, 128:] for a, b in zip(rest, (out, gq, gk, gv))]
        att[rows, MAIN:] = rest[0].astype(BF16)
        dq[rows, MAIN:] = rest[1].astype(BF16)
        dk[rows, MAIN:] = rest[2].astype(BF16)
        dqkv[rows, QK + MAIN :] = rest[3].astype(BF16)

    over_rows(ROWS, attend)

    def out_project(first, size):
        cols = slice(first, first + size)
        y = dot(att[...], wout[:, cols])
        sums[2:3, cols] = jnp.sum(cp[:, cols] * y, 0, keepdims=True)
        value = xp[:, cols] + mod_ref[2:3, cols] * y
        for c in range(size // LANES):
            for p in range(POS):
                frames[first // LANES + c, at_position(p), :] = value[
                    p * FR : (p + 1) * FR, c * LANES : (c + 1) * LANES
                ]

    for first in range(0, D, 384):
        out_project(first, 384)
    drain(0)

    def heads_grad(rows):
        for part, (d_ref, r_ref) in enumerate(((dq, rq), (dk, rk))):
            main = slice(MAIN_AT[part], MAIN_AT[part] + MAIN)
            rest = slice(REST_AT[part], REST_AT[part] + REST)
            gain = gain_ref[part : part + 1, :]
            row = slice(3 + part, 4 + part)
            um, ur = d_ref[rows, :MAIN].astype(F32), d_ref[rows, MAIN:].astype(F32)
            wm, wr = um * proj[rows, main], ur * proj[rows, rest]
            sums[row, :MAIN] += jnp.sum(wm, 0, keepdims=True)
            sums[row, MAIN:] += jnp.sum(wr, 0, keepdims=True)
            total = dot((wm * gain[:, :MAIN]).astype(BF16), seg[:MAIN, :]) + dot(
                (wr * gain[:, MAIN:]).astype(BF16), seg[MAIN:, :]
            )
            inner = total * (1.0 / HEAD)
            inv = r_ref[rows, :]
            pair, inner_pair = both(inv), both(inner)
            for b in range(0, MAIN, 256):
                cols = slice(MAIN_AT[part] + b, MAIN_AT[part] + b + 256)
                a = d_ref[rows, b : b + 256].astype(F32) * gain[:, b : b + 256]
                picked = spread[:, b : b + 256]
                value = dot(pair, picked) * (a - proj[rows, cols] * dot(inner_pair, picked))
                dqkv[rows, cols] = value.astype(BF16)
            value = inv * (ur * gain[:, MAIN:] - proj[rows, rest] * inner)
            dqkv[rows, rest] = value.astype(BF16)

    over_rows(256, heads_grad)

    def grad_normed(cols):
        gn[:, cols] = dot(dqkv[...], wqkv[cols, :], NT).astype(BF16)

    over_columns(D, grad_normed)

    def layer(p):
        rows = position_rows(p)
        grads = [gn[rows, cols].astype(F32) for cols in lane_tiles()]
        units = [unit[rows, cols] for cols in lane_tiles()]
        scaled = []
        for g, u, cols in zip(grads, units, lane_tiles()):
            sums[0:1, cols] += jnp.sum(g, 0, keepdims=True)
            sums[1:2, cols] += jnp.sum(g * u, 0, keepdims=True)
            scaled.append(g * (1.0 + mod_ref[1:2, cols]))
        first = jnp.sum(sum(scaled), -1, keepdims=True) * (1.0 / D)
        second = jnp.sum(sum(g * u for g, u in zip(scaled, units)), -1, keepdims=True) * (1.0 / D)
        inv = istd[rows, :]
        for c, cols in enumerate(lane_tiles()):
            frames[c, at_position(p), :] = cp[rows, cols] + inv * (
                scaled[c] - first - units[c] * second
            )

    loop(POS, layer)
    drain(16)

    total = sums[...]
    folded = sum(dot(part, fold[...]) for part in terms(total))
    gains = jnp.concatenate([folded[3:4], folded[4:5], jnp.zeros((1, D - 256), F32)], 1)
    total = jnp.concatenate([total[:3], gains], 0)
    rows = jnp.concatenate([part.astype(F32) for part in terms(total)] + [jnp.zeros((4, D), F32)], 0)
    out_ref[:, 32:, :] = jnp.broadcast_to(rows.astype(BF16)[None], (ranks, SUMS, D))


def run_sub_block(frame_counts, arrived, modulation, gains, wqkv, wout):
    ranks = arrived.shape[0]
    tok = (TOK, D)
    any_space = pl.BlockSpec(memory_space=pl.ANY)
    vmem = pl.BlockSpec(memory_space=pltpu.VMEM)
    scratch = [
        pltpu.VMEM((D, 3 * D), BF16),
        pltpu.VMEM((D, D), BF16),
        pltpu.SemaphoreType.DMA((2,)),
        pltpu.VMEM((TILES, TOK, LANES), F32),
        pltpu.VMEM(tok, F32),
        pltpu.VMEM(tok, F32),
        pltpu.VMEM((TOK, LANES), F32),
        pltpu.VMEM(tok, F32),
        pltpu.VMEM(tok, BF16),
        pltpu.VMEM(tok, BF16),
        pltpu.VMEM((TOK, QK), F32),
        pltpu.VMEM(tok, BF16),
        pltpu.VMEM(tok, BF16),
        pltpu.VMEM(tok, BF16),
        pltpu.VMEM(tok, BF16),
        pltpu.VMEM((TOK, REST), F32),
        pltpu.VMEM((TOK, REST), F32),
        pltpu.VMEM(tok, BF16),
        pltpu.VMEM(tok, BF16),
        pltpu.VMEM((TOK, 3 * D), BF16),
        pltpu.VMEM((8, D), F32),
        pltpu.VMEM((D, REST), BF16),
        pltpu.VMEM((2 * REST, MAIN), BF16),
        pltpu.VMEM((D, REST), BF16),
        pltpu.VMEM((128, 128), F32),
    ]
    return pl.pallas_call(
        sub_block,
        in_specs=[pl.BlockSpec(memory_space=pltpu.SMEM), vmem, vmem, vmem, any_space, any_space],
        out_specs=vmem,
        out_shape=jax.ShapeDtypeStruct((ranks, SENT, D), BF16),
        scratch_shapes=scratch,
        compiler_params=pltpu.CompilerParams(vmem_limit_bytes=VMEM),
        cost_estimate=pl.CostEstimate(
            flops=17_000_000_000, bytes_accessed=20_000_000, transcendentals=0
        ),
        name="sub_block",
    )(frame_counts, arrived, modulation, gains, wqkv, wout)


def sum_over(value, axis, size):
    step = 1
    while step < size:
        value = value + lax.ppermute(value, axis, [(i, i ^ step) for i in range(size)])
        step *= 2
    return value


def split_gain(gain):
    return jnp.concatenate([jnp.tile(gain[:64], HEADS), jnp.tile(gain[64:], HEADS)])


def shards(latents, frame_counts, mod_table, clip_mod, q_gain, k_gain, w_qkv, w_out, cotangent):
    ranks = lax.axis_size("seq")
    modulation = mod_table + clip_mod[0]
    gains = jnp.stack([split_gain(q_gain), split_gain(k_gain)])

    def exchange(rows):
        return lax.all_to_all(rows, "seq", split_axis=0, concat_axis=0, tiled=True)

    def outgoing(array):
        return array.reshape(2, ranks, POS, D).transpose(1, 0, 2, 3).reshape(ranks, 16, D)

    def incoming(array):
        return array.reshape(ranks, 2, POS, D).transpose(1, 0, 2, 3).reshape(latents.shape)

    arrived = exchange(jnp.concatenate([outgoing(latents), outgoing(cotangent)], 1))
    wqkv, wout = split_weights(w_qkv, w_out)
    out = run_sub_block(frame_counts, arrived, modulation, gains, wqkv, wout)
    back = exchange(out)
    pieces = jnp.sum(back[:, 32:, :].astype(F32), 0)
    clip_total = pieces[0:4] + pieces[4:8] + pieces[8:12]
    total = sum_over(clip_total, "dp", lax.axis_size("dp"))
    return (
        incoming(back[:, :16, :]),
        incoming(back[:, 16:32, :]),
        clip_total[None, :3],
        total[:3],
        total[3, :HEAD],
        total[3, 128 : 128 + HEAD],
    )


def solution(mesh):
    return jax.shard_map(
        shards,
        mesh=mesh,
        in_specs=(
            P("dp", "seq", None, None),
            P("dp"),
            P(),
            P("dp", None, None),
            P(),
            P(),
            P(),
            P(),
            P("dp", "seq", None, None),
        ),
        out_specs=(
            P("dp", "seq", None, None),
            P("dp", "seq", None, None),
            P("dp", None, None),
            P(),
            P(),
            P(),
        ),
        check_vma=False,
    )
```

```python
import functools

import jax
import jax.numpy as jnp
from jax import lax
from jax.experimental import pallas as pl
from jax.experimental.pallas import tpu as pltpu
from jax.sharding import PartitionSpec as P

EPS = 1e-06
F32 = jnp.float32
BF16 = jnp.bfloat16
HEAD = 72
HEADS = 16
D = HEAD * HEADS
MAIN = 64 * HEADS
REST = 8 * HEADS
QK = 2 * D
MAIN_AT = (0, MAIN, QK)
REST_AT = (2 * MAIN, 2 * MAIN + REST, QK + MAIN)
CHUNKS = 2
POS = 4
FR = 64
TOK = POS * FR
ROWS = 128
PAIRS = TOK // ROWS
BLOCK = 512
LANES = 128
TILES = D // LANES
ROWS_IN = 16
SUMS = 8
VMEM = 56 * 1024 * 1024
NN = (((1,), (0,)), ((), ()))
NT = (((1,), (1,)), ((), ()))
TN = (((0,), (0,)), ((), ()))


def dot(a, b, dims=NN):
    return lax.dot_general(a, b, dims, preferred_element_type=F32)


def iota(shape, dim):
    return lax.broadcasted_iota(jnp.int32, shape, dim)


def one_hot(cond):
    return jnp.where(cond, jnp.float32(1), jnp.float32(0)).astype(BF16)


def source_main(col):
    return col + 8 * (col >> 6)


def source_rest(col):
    return col + 64 + 64 * (col >> 3)


def window(j):
    return 288 * j // 128 * 128


def split_weights_kernel(qkv_ref, out_ref, qkv_o, out_o, pick, pick_rest):
    @pl.when(pl.program_id(0) == 0)
    def _():
        for j in range(4):
            r, c = iota((384, 256), 0), iota((384, 256), 1)
            pick[j] = one_hot(source_main(c + 256 * j) == r + window(j))
        r, c = iota((D, REST), 0), iota((D, REST), 1)
        pick_rest[...] = one_hot(source_rest(c) == r)

    for part in range(3):
        base = part * D
        for j in range(4):
            lo = base + window(j)
            qkv_o[:, MAIN_AT[part] + 256 * j : MAIN_AT[part] + 256 * (j + 1)] = dot(
                qkv_ref[:, lo : lo + 384], pick[j]
            ).astype(BF16)
        qkv_o[:, REST_AT[part] : REST_AT[part] + REST] = dot(
            qkv_ref[:, base : base + D], pick_rest[...]
        ).astype(BF16)

    for j in range(4):
        out_o[256 * j : 256 * (j + 1), :] = dot(
            pick[j], out_ref[window(j) : window(j) + 384, :], TN
        ).astype(BF16)
    out_o[MAIN:, :] = dot(pick_rest[...], out_ref[...], TN).astype(BF16)


def split_weights(w_qkv, w_out):
    steps = 3
    part = D // steps
    return pl.pallas_call(
        split_weights_kernel,
        grid=(steps,),
        in_specs=[
            pl.BlockSpec((part, 3 * D), lambda i: (i, 0)),
            pl.BlockSpec((D, part), lambda i: (0, i)),
        ],
        out_specs=[
            pl.BlockSpec((part, 3 * D), lambda i: (i, 0)),
            pl.BlockSpec((D, part), lambda i: (0, i)),
        ],
        out_shape=[
            jax.ShapeDtypeStruct((D, 3 * D), BF16),
            jax.ShapeDtypeStruct((D, D), BF16),
        ],
        scratch_shapes=[pltpu.VMEM((4, 384, 256), BF16), pltpu.VMEM((D, REST), BF16)],
        compiler_params=pltpu.CompilerParams(vmem_limit_bytes=VMEM),
        cost_estimate=pl.CostEstimate(
            flops=2 * D * D * 1600, bytes_accessed=16 * D * D, transcendentals=0
        ),
        name="split_weights",
    )(w_qkv, w_out)


def trade(first, second, chunk):
    upper = iota(first.shape, 1) < POS
    if chunk == 0:
        return jnp.where(upper, first, pltpu.roll(second, POS, 1))
    return jnp.where(upper, pltpu.roll(first, POS, 1), second)


def pack_kernel(chunk, lat_ref, cot_ref, *refs):
    o_ref = refs[-1]
    ranks, _, width = o_ref.shape
    for c in range(TILES):
        cols = slice(LANES * c, LANES * (c + 1))
        halves = []
        for ref in (lat_ref, cot_ref):
            tiles = [ref[0, i, :, cols].astype(F32).reshape(ranks, 8, LANES) for i in range(2)]
            halves.append(trade(*tiles, chunk))
        o_ref[:, :, cols] = jnp.concatenate(halves, 1).astype(BF16)


def pack(latents, cotangent, chunk, after=()):
    _, frames, positions, width = latents.shape
    steps = 4
    ranks = positions // 8
    spec = pl.BlockSpec((1, frames, positions // steps, width), lambda i: (0, 0, i, 0))
    return pl.pallas_call(
        functools.partial(pack_kernel, chunk),
        grid=(steps,),
        in_specs=[spec, spec] + [pl.BlockSpec(memory_space=pl.ANY)] * len(after),
        out_specs=pl.BlockSpec((ranks // steps, ROWS_IN, width), lambda i: (i, 0, 0)),
        out_shape=jax.ShapeDtypeStruct((ranks, ROWS_IN, width), BF16),
        compiler_params=pltpu.CompilerParams(vmem_limit_bytes=VMEM),
        cost_estimate=pl.CostEstimate(flops=4_000_000, bytes_accessed=3_600_000, transcendentals=0),
        name="pack",
    )(latents, cotangent, *after)


def tie_kernel(value_ref, other_ref, o_ref):
    del value_ref, other_ref, o_ref


def tie(value, other):
    any_space = pl.BlockSpec(memory_space=pl.ANY)
    return pl.pallas_call(
        tie_kernel,
        in_specs=[any_space, any_space],
        out_specs=any_space,
        out_shape=jax.ShapeDtypeStruct(value.shape, value.dtype),
        input_output_aliases={0: 0},
        name="tie",
    )(value, other)


def unpack_kernel(first_ref, second_ref, block_ref, grad_ref):
    ranks = first_ref.shape[0]
    for c in range(TILES):
        cols = slice(LANES * c, LANES * (c + 1))
        first, second = first_ref[:, :, cols].astype(F32), second_ref[:, :, cols].astype(F32)
        for at, ref in ((0, block_ref), (8, grad_ref)):
            for i in range(2):
                tile = trade(first[:, at : at + 8], second[:, at : at + 8], i)
                ref[0, i, :, cols] = tile.reshape(ranks * 8, LANES).astype(BF16)


def unpack(first, second, shape):
    _, frames, positions, width = shape
    steps = 4
    spec = pl.BlockSpec((1, frames, positions // steps, width), lambda i: (0, 0, i, 0))
    out = jax.ShapeDtypeStruct(shape, BF16)
    return pl.pallas_call(
        unpack_kernel,
        grid=(steps,),
        in_specs=[
            pl.BlockSpec((x.shape[0] // steps, *x.shape[1:]), lambda i: (i, 0, 0))
            for x in (first, second)
        ],
        out_specs=[spec, spec],
        out_shape=[out, out],
        compiler_params=pltpu.CompilerParams(vmem_limit_bytes=VMEM),
        cost_estimate=pl.CostEstimate(flops=4_000_000, bytes_accessed=5_000_000, transcendentals=0),
        name="unpack",
    )(first, second)


def init_segments(seg, spread, fold):
    r, c = iota((D, REST), 0), iota((D, REST), 1)
    head = jnp.where(r < MAIN, r >> 6, (r - MAIN) >> 3)
    seg[...] = one_hot(head == (c >> 3))
    entry = jnp.where(r < MAIN, r & 63, 64 + (r & 7))
    fold[...] = one_hot(entry == c)
    r, c = iota((2 * REST, MAIN), 0), iota((2 * REST, MAIN), 1)
    spread[...] = one_hot((r & (REST - 1)) == 8 * (c >> 6))


def terms(value):
    high = value.astype(BF16)
    left = value - high.astype(F32)
    mid = left.astype(BF16)
    return high, mid, (left - mid.astype(F32)).astype(BF16)


def both(per_head):
    high = per_head.astype(BF16)
    return jnp.concatenate([high, (per_head - high.astype(F32)).astype(BF16)], 1)


def head_masks(t):
    c = iota((1, 256), 1)
    head = jnp.where(c < 128, (c >> 6) + 2 * t, (c - 128) >> 3)
    return [one_hot(head == h) for h in (2 * t, 2 * t + 1)]


def unit_of(ref, rows, t):
    return jnp.concatenate([ref[rows, 128 * t : 128 * (t + 1)], ref[rows, MAIN:]], 1)


def stacked(block, masks):
    return [
        jnp.concatenate([block[:FR] * masks[0], block[:FR] * masks[1]], 0),
        jnp.concatenate([block[FR:] * masks[0], block[FR:] * masks[1]], 0),
    ]


def diagonal(block):
    zero = jnp.zeros((FR, 256), BF16)
    return jnp.concatenate(
        [
            jnp.concatenate([block[:FR], zero], 1),
            jnp.concatenate([zero, block[FR:]], 1),
        ],
        0,
    )


def by_position(block):
    lane, zero = iota((128, 128), 1), jnp.zeros((128, 128), F32)
    own = lane < FR
    return jnp.concatenate(
        [jnp.where(own, block, zero), jnp.where(own, zero, block)], 0
    ).astype(BF16)


def own_rows(product, masks):
    zero, one = masks[0].astype(F32), masks[1].astype(F32)
    return jnp.concatenate(
        [
            product[:64] * zero + product[64:128] * one,
            product[128:192] * zero + product[192:] * one,
        ],
        0,
    )


def loop(count, body):
    def step(i, _):
        body(i)
        return 0

    lax.fori_loop(0, count, step, 0)


def over_columns(total, body):
    loop(total // BLOCK, lambda b: body(pl.ds(pl.multiple_of(b * BLOCK, BLOCK), BLOCK)))
    if total % BLOCK:
        body(pl.ds(total // BLOCK * BLOCK, total % BLOCK))


def over_rows(size, body):
    loop(TOK // size, lambda i: body(pl.ds(pl.multiple_of(i * size, size), size)))


def lane_tiles():
    return [slice(LANES * c, LANES * (c + 1)) for c in range(TILES)]


def sub_block(
    last,
    count_ref,
    in_hbm,
    table_ref,
    clip_ref,
    q_gain_ref,
    k_gain_ref,
    wqkv_hbm,
    wout_hbm,
    before_ref,
    out_ref,
    sums,
    in_ref,
    wqkv,
    wout,
    sems,
    frames,
    xp,
    unit,
    istd,
    cp,
    gy,
    normed,
    proj,
    gatt,
    qn,
    kn,
    vn,
    rq,
    rk,
    dq,
    dk,
    dqkv,
    seg,
    spread,
    fold,
    bias,
    mod_ref,
    gain_ref,
):
    ranks = in_ref.shape[0]
    att, gn = gy, normed
    load_qkv = pltpu.make_async_copy(wqkv_hbm, wqkv, sems.at[0])
    load_out = pltpu.make_async_copy(wout_hbm, wout, sems.at[1])
    load_in = pltpu.make_async_copy(in_hbm, in_ref, sems.at[2])
    load_in.start()
    load_out.start()
    load_qkv.start()
    init_segments(seg, spread, fold)
    key = iota((128, 128), 0) & (FR - 1)
    valid = 2 * (key & 31) + (key >> 5) < count_ref[0]
    bias[...] = jnp.where(valid, jnp.float32(0), jnp.float32(-1e30))
    sums[...] = before_ref[...]
    mod_ref[...] = table_ref[...] + clip_ref[...]
    for part, ref in enumerate((q_gain_ref, k_gain_ref)):
        gain_ref[part : part + 1, :] = sum(dot(x, fold[:, :HEAD], NT) for x in terms(ref[...]))

    def strided(p, first, own):
        return pl.ds(first + own * POS + p, ranks, stride=ROWS_IN)

    def gather(c, p, first):
        return jnp.concatenate([frames[c, strided(p, first, own), :] for own in range(2)], 0)

    def scatter(c, p, first, value):
        for own in range(2):
            frames[c, strided(p, first, own), :] = value[own * ranks : (own + 1) * ranks]

    def position_rows(p):
        return pl.ds(pl.multiple_of(p * FR, FR), FR)

    load_in.wait()
    for c, cols in enumerate(lane_tiles()):
        frames[c] = in_ref[:, :, cols].reshape(ranks * ROWS_IN, LANES).astype(F32)

    def arrive(p):
        rows = position_rows(p)
        for c, cols in enumerate(lane_tiles()):
            cot = gather(c, p, 8)
            cp[rows, cols] = cot
            gy[rows, cols] = (cot * mod_ref[2:3, cols]).astype(BF16)

    def norm(p):
        rows = position_rows(p)
        parts = [gather(c, p, 0) for c in range(TILES)]
        mean = jnp.sum(sum(parts), -1, keepdims=True) * (1.0 / D)
        centred = [x - mean for x in parts]
        square = jnp.sum(sum(x * x for x in centred), -1, keepdims=True) * (1.0 / D)
        inv = lax.rsqrt(square + EPS)
        istd[rows, :] = jnp.broadcast_to(inv, (FR, LANES))
        for c, cols in enumerate(lane_tiles()):
            xp[rows, cols] = parts[c]
            u = centred[c] * inv
            unit[rows, cols] = u
            normed[rows, cols] = (u * (1.0 + mod_ref[1:2, cols]) + mod_ref[0:1, cols]).astype(BF16)

    loop(POS, arrive)
    loop(POS, norm)

    def grad_attention(cols):
        gatt[:, cols] = dot(gy[...], wout[cols, :], NT).astype(BF16)

    load_out.wait()
    over_columns(D, grad_attention)

    def project(cols):
        proj[:, cols] = dot(normed[...], wqkv[:, cols])

    load_qkv.wait()
    over_columns(QK, project)

    def project_values(cols):
        vn[:, cols] = dot(normed[...], wqkv[:, pl.ds(QK + cols.start, cols.size)]).astype(BF16)

    over_columns(D, project_values)

    def heads(rows):
        for part, (n_ref, r_ref) in enumerate(((qn, rq), (kn, rk))):
            main = slice(MAIN_AT[part], MAIN_AT[part] + MAIN)
            rest = slice(REST_AT[part], REST_AT[part] + REST)
            m, t = proj[rows, main], proj[rows, rest]
            total = sum(dot(part, seg[:MAIN, :]) for part in terms(m * m)[:2])
            total = total + sum(dot(part, seg[MAIN:, :]) for part in terms(t * t)[:2])
            inv = lax.rsqrt(total * (1.0 / HEAD) + EPS)
            r_ref[rows, :] = inv
            pair = both(inv)
            for b in range(0, MAIN, 256):
                cols = slice(MAIN_AT[part] + b, MAIN_AT[part] + b + 256)
                hat = proj[rows, cols] * dot(pair, spread[:, b : b + 256])
                proj[rows, cols] = hat
                n_ref[rows, b : b + 256] = (hat * gain_ref[part : part + 1, b : b + 256]).astype(BF16)
            hat = t * inv
            proj[rows, rest] = hat
            n_ref[rows, MAIN:] = (hat * gain_ref[part : part + 1, MAIN:]).astype(BF16)

    over_rows(256, heads)

    def attend(rows):
        rest = [jnp.zeros((ROWS, REST), F32)] * 4
        ops, soft = [], []
        for t in range(HEADS // 2):
            masks = head_masks(t)
            keys = stacked(unit_of(kn, rows, t), masks)
            vals = stacked(unit_of(vn, rows, t), masks)
            query = diagonal(unit_of(qn, rows, t))
            grad = diagonal(unit_of(gatt, rows, t))
            s = dot(jnp.concatenate(keys, 1), query, NT) * (HEAD**-0.5) + bias[...]
            dp = dot(jnp.concatenate(vals, 1), grad, NT)
            ops.append((t, masks, keys, vals, s, dp))
        for *_, s, dp in ops:
            s, dp = s.reshape(2, FR, 128), dp.reshape(2, FR, 128)
            e = jnp.exp(s - jnp.max(s, 1, keepdims=True))
            prob = e * (1.0 / jnp.sum(e, 1, keepdims=True))
            delta = jnp.sum(prob * dp, 1, keepdims=True)
            ds = (prob * (dp - delta) * (HEAD**-0.5)).reshape(128, 128)
            prob = prob.reshape(128, 128)
            soft.append((prob, ds))
        for (t, masks, keys, vals, _, _), (prob, ds) in zip(ops, soft):
            pt, dt = prob.T.astype(BF16), ds.T.astype(BF16)
            cols = slice(128 * t, 128 * (t + 1))
            out = jnp.concatenate([dot(pt[:FR], vals[0]), dot(pt[FR:], vals[1])], 0)
            gq = jnp.concatenate([dot(dt[:FR], keys[0]), dot(dt[FR:], keys[1])], 0)
            gk = own_rows(dot(by_position(ds), unit_of(qn, rows, t)), masks)
            gv = own_rows(dot(by_position(prob), unit_of(gatt, rows, t)), masks)
            att[rows, cols] = out[:, :128].astype(BF16)
            dq[rows, cols] = gq[:, :128].astype(BF16)
            dk[rows, cols] = gk[:, :128].astype(BF16)
            dqkv[rows, QK + 128 * t : QK + 128 * (t + 1)] = gv[:, :128].astype(BF16)
            rest = [a + b[:, 128:] for a, b in zip(rest, (out, gq, gk, gv))]
        att[rows, MAIN:] = rest[0].astype(BF16)
        dq[rows, MAIN:] = rest[1].astype(BF16)
        dk[rows, MAIN:] = rest[2].astype(BF16)
        dqkv[rows, QK + MAIN :] = rest[3].astype(BF16)

    over_rows(ROWS, attend)

    def out_project(first, size):
        cols = slice(first, first + size)
        y = dot(att[...], wout[:, cols])
        sums[2:3, cols] += jnp.sum(cp[:, cols] * y, 0, keepdims=True)
        value = xp[:, cols] + mod_ref[2:3, cols] * y
        for c in range(size // LANES):
            for p in range(POS):
                tile = value[p * FR : (p + 1) * FR, c * LANES : (c + 1) * LANES]
                scatter(first // LANES + c, p, 0, tile)

    for first in range(0, D, BLOCK):
        out_project(first, min(BLOCK, D - first))

    def heads_grad(rows):
        for part, (d_ref, r_ref) in enumerate(((dq, rq), (dk, rk))):
            main = slice(MAIN_AT[part], MAIN_AT[part] + MAIN)
            rest = slice(REST_AT[part], REST_AT[part] + REST)
            gain = gain_ref[part : part + 1, :]
            row = slice(3 + part, 4 + part)
            um, ur = d_ref[rows, :MAIN].astype(F32), d_ref[rows, MAIN:].astype(F32)
            wm, wr = um * proj[rows, main], ur * proj[rows, rest]
            sums[row, :MAIN] += jnp.sum(wm, 0, keepdims=True)
            sums[row, MAIN:] += jnp.sum(wr, 0, keepdims=True)
            total = dot((wm * gain[:, :MAIN]).astype(BF16), seg[:MAIN, :]) + dot(
                (wr * gain[:, MAIN:]).astype(BF16), seg[MAIN:, :]
            )
            inner = total * (1.0 / HEAD)
            inv = r_ref[rows, :]
            pair, inner_pair = both(inv), both(inner)
            for b in range(0, MAIN, 256):
                cols = slice(MAIN_AT[part] + b, MAIN_AT[part] + b + 256)
                a = d_ref[rows, b : b + 256].astype(F32) * gain[:, b : b + 256]
                picked = spread[:, b : b + 256]
                value = dot(pair, picked) * (a - proj[rows, cols] * dot(inner_pair, picked))
                dqkv[rows, cols] = value.astype(BF16)
            value = inv * (ur * gain[:, MAIN:] - proj[rows, rest] * inner)
            dqkv[rows, rest] = value.astype(BF16)

    over_rows(256, heads_grad)

    def grad_normed(cols):
        gn[:, cols] = dot(dqkv[...], wqkv[cols, :], NT).astype(BF16)

    over_columns(D, grad_normed)

    def layer(p):
        rows = position_rows(p)
        grads = [gn[rows, cols].astype(F32) for cols in lane_tiles()]
        units = [unit[rows, cols] for cols in lane_tiles()]
        scaled = []
        for g, u, cols in zip(grads, units, lane_tiles()):
            sums[0:1, cols] += jnp.sum(g, 0, keepdims=True)
            sums[1:2, cols] += jnp.sum(g * u, 0, keepdims=True)
            scaled.append(g * (1.0 + mod_ref[1:2, cols]))
        first = jnp.sum(sum(scaled), -1, keepdims=True) * (1.0 / D)
        second = jnp.sum(sum(g * u for g, u in zip(scaled, units)), -1, keepdims=True) * (1.0 / D)
        inv = istd[rows, :]
        for c, cols in enumerate(lane_tiles()):
            value = cp[rows, cols] + inv * (scaled[c] - first - units[c] * second)
            scatter(c, p, 8, value)

    loop(POS, layer)

    if last:
        total = sums[...]
        folded = sum(dot(part, fold[...]) for part in terms(total))
        gains = jnp.concatenate([folded[3:4], folded[4:5], jnp.zeros((1, D - 256), F32)], 1)
        high, low, _ = terms(jnp.concatenate([total[:3], gains], 0))
        sent = jnp.concatenate([high.astype(F32), low.astype(F32)], 0)
    for c, cols in enumerate(lane_tiles()):
        block = frames[c].reshape(ranks, ROWS_IN, LANES)
        if last:
            rows = jnp.broadcast_to(sent[None, :, cols], (ranks, SUMS, LANES))
            block = jnp.concatenate([block, rows], 1)
        out_ref[:, :, cols] = block.astype(BF16)


def run_sub_block(last, frame_counts, arrived, modulation, gains, weights, before):
    ranks = arrived.shape[0]
    tok = (TOK, D)
    any_space = pl.BlockSpec(memory_space=pl.ANY)
    vmem = pl.BlockSpec(memory_space=pltpu.VMEM)
    scratch = [
        pltpu.VMEM((ranks, ROWS_IN, D), BF16),
        pltpu.VMEM((D, 3 * D), BF16),
        pltpu.VMEM((D, D), BF16),
        pltpu.SemaphoreType.DMA((3,)),
        pltpu.VMEM((TILES, ranks * ROWS_IN, LANES), F32),
        pltpu.VMEM(tok, F32),
        pltpu.VMEM(tok, F32),
        pltpu.VMEM((TOK, LANES), F32),
        pltpu.VMEM(tok, F32),
        pltpu.VMEM(tok, BF16),
        pltpu.VMEM(tok, BF16),
        pltpu.VMEM((TOK, QK), F32),
        pltpu.VMEM(tok, BF16),
        pltpu.VMEM(tok, BF16),
        pltpu.VMEM(tok, BF16),
        pltpu.VMEM(tok, BF16),
        pltpu.VMEM((TOK, REST), F32),
        pltpu.VMEM((TOK, REST), F32),
        pltpu.VMEM(tok, BF16),
        pltpu.VMEM(tok, BF16),
        pltpu.VMEM((TOK, 3 * D), BF16),
        pltpu.VMEM((D, REST), BF16),
        pltpu.VMEM((2 * REST, MAIN), BF16),
        pltpu.VMEM((D, REST), BF16),
        pltpu.VMEM((128, 128), F32),
        pltpu.VMEM((3, D), F32),
        pltpu.VMEM((2, D), F32),
    ]
    sent = ROWS_IN + SUMS if last else ROWS_IN
    return pl.pallas_call(
        functools.partial(sub_block, last),
        in_specs=[pl.BlockSpec(memory_space=pltpu.SMEM)]
        + [any_space]
        + [vmem] * 4
        + [any_space, any_space, vmem],
        out_specs=[vmem, vmem],
        out_shape=[
            jax.ShapeDtypeStruct((ranks, sent, D), BF16),
            jax.ShapeDtypeStruct((8, D), F32),
        ],
        scratch_shapes=scratch,
        compiler_params=pltpu.CompilerParams(vmem_limit_bytes=VMEM),
        cost_estimate=pl.CostEstimate(
            flops=12_000_000_000, bytes_accessed=20_000_000, transcendentals=0
        ),
        name="sub_block",
    )(frame_counts, arrived, *modulation, *gains, *weights, before)


def sum_clips(value):
    clips = lax.axis_size("dp")
    one, two, three = (
        lax.ppermute(value, "dp", [(i, i ^ step) for i in range(clips)]) for step in (1, 2, 3)
    )
    return (value + one) + (two + three)


def shards(latents, frame_counts, mod_table, clip_mod, q_gain, k_gain, w_qkv, w_out, cotangent):
    ranks = lax.axis_size("seq")
    modulation = (mod_table, clip_mod[0])
    gains = (q_gain[None], k_gain[None])

    def exchange(rows):
        return lax.all_to_all(rows, "seq", split_axis=0, concat_axis=0, tiled=True)

    weights = split_weights(w_qkv, w_out)
    arrived = [
        exchange(pack(latents, cotangent, 0)),
        exchange(pack(latents, cotangent, 1, after=weights[1:])),
    ]
    sums = jnp.zeros((8, D), F32)
    back = []
    for i in range(CHUNKS):
        last = i == CHUNKS - 1
        out, sums = run_sub_block(last, frame_counts, arrived[i], modulation, gains, weights, sums)
        back.append(exchange(tie(out, back[0]) if last else out))
    pieces = jnp.sum(back[-1][:, ROWS_IN:, :].astype(F32), 0)
    clip_total = pieces[0:4] + pieces[4:8]
    total = sum_clips(clip_total)
    block_out, input_grad = unpack(*back, latents.shape)
    return (
        block_out,
        input_grad,
        clip_total[None, :3],
        total[:3],
        total[3, :HEAD],
        total[3, 128 : 128 + HEAD],
    )


def solution(mesh):
    return jax.shard_map(
        shards,
        mesh=mesh,
        in_specs=(
            P("dp", "seq", None, None),
            P("dp"),
            P(),
            P("dp", None, None),
            P(),
            P(),
            P(),
            P(),
            P("dp", "seq", None, None),
        ),
        out_specs=(
            P("dp", "seq", None, None),
            P("dp", "seq", None, None),
            P("dp", None, None),
            P(),
            P(),
            P(),
        ),
        check_vma=False,
    )
```

```python
import functools

import jax
import jax.numpy as jnp
from jax import lax
from jax.experimental import pallas as pl
from jax.experimental.pallas import tpu as pltpu
from jax.sharding import PartitionSpec as P

EPS = 1e-06
F32 = jnp.float32
BF16 = jnp.bfloat16
HEAD = 72
HEADS = 16
D = HEAD * HEADS
MAIN = 64 * HEADS
REST = 8 * HEADS
QK = 2 * D
MAIN_AT = (0, MAIN, QK)
REST_AT = (2 * MAIN, 2 * MAIN + REST, QK + MAIN)
CHUNKS = 2
POS = 4
FR = 64
TOK = POS * FR
ROWS = 128
PAIRS = TOK // ROWS
BLOCK = 512
LANES = 128
TILES = D // LANES
ROWS_IN = 16
SUMS = 8
VMEM = 56 * 1024 * 1024
NN = (((1,), (0,)), ((), ()))
NT = (((1,), (1,)), ((), ()))
TN = (((0,), (0,)), ((), ()))


def dot(a, b, dims=NN):
    return lax.dot_general(a, b, dims, preferred_element_type=F32)


def iota(shape, dim):
    return lax.broadcasted_iota(jnp.int32, shape, dim)


def one_hot(cond):
    return jnp.where(cond, jnp.float32(1), jnp.float32(0)).astype(BF16)


def source_main(col):
    return col + 8 * (col >> 6)


def source_rest(col):
    return col + 64 + 64 * (col >> 3)


def window(j):
    return 288 * j // 128 * 128


def split_weights_kernel(qkv_ref, out_ref, qkv_o, out_o, pick, pick_rest):
    @pl.when(pl.program_id(0) == 0)
    def _():
        for j in range(4):
            r, c = iota((384, 256), 0), iota((384, 256), 1)
            pick[j] = one_hot(source_main(c + 256 * j) == r + window(j))
        r, c = iota((D, REST), 0), iota((D, REST), 1)
        pick_rest[...] = one_hot(source_rest(c) == r)

    for part in range(3):
        base = part * D
        for j in range(4):
            lo = base + window(j)
            qkv_o[:, MAIN_AT[part] + 256 * j : MAIN_AT[part] + 256 * (j + 1)] = dot(
                qkv_ref[:, lo : lo + 384], pick[j]
            ).astype(BF16)
        qkv_o[:, REST_AT[part] : REST_AT[part] + REST] = dot(
            qkv_ref[:, base : base + D], pick_rest[...]
        ).astype(BF16)

    for j in range(4):
        out_o[256 * j : 256 * (j + 1), :] = dot(
            pick[j], out_ref[window(j) : window(j) + 384, :], TN
        ).astype(BF16)
    out_o[MAIN:, :] = dot(pick_rest[...], out_ref[...], TN).astype(BF16)


def split_weights(w_qkv, w_out):
    steps = 3
    part = D // steps
    return pl.pallas_call(
        split_weights_kernel,
        grid=(steps,),
        in_specs=[
            pl.BlockSpec((part, 3 * D), lambda i: (i, 0)),
            pl.BlockSpec((D, part), lambda i: (0, i)),
        ],
        out_specs=[
            pl.BlockSpec((part, 3 * D), lambda i: (i, 0)),
            pl.BlockSpec((D, part), lambda i: (0, i)),
        ],
        out_shape=[
            jax.ShapeDtypeStruct((D, 3 * D), BF16),
            jax.ShapeDtypeStruct((D, D), BF16),
        ],
        scratch_shapes=[pltpu.VMEM((4, 384, 256), BF16), pltpu.VMEM((D, REST), BF16)],
        compiler_params=pltpu.CompilerParams(vmem_limit_bytes=VMEM),
        cost_estimate=pl.CostEstimate(
            flops=2 * D * D * 1600, bytes_accessed=16 * D * D, transcendentals=0
        ),
        name="split_weights",
    )(w_qkv, w_out)


def trade(first, second, chunk):
    upper = iota(first.shape, 1) < POS
    if chunk == 0:
        return jnp.where(upper, first, pltpu.roll(second, POS, 1))
    return jnp.where(upper, pltpu.roll(first, POS, 1), second)


def pack_kernel(chunk, lat_ref, cot_ref, *refs):
    o_ref = refs[-1]
    ranks, _, width = o_ref.shape
    for c in range(TILES):
        cols = slice(LANES * c, LANES * (c + 1))
        halves = []
        for ref in (lat_ref, cot_ref):
            tiles = [ref[0, i, :, cols].astype(F32).reshape(ranks, 8, LANES) for i in range(2)]
            halves.append(trade(*tiles, chunk))
        o_ref[:, :, cols] = jnp.concatenate(halves, 1).astype(BF16)


def pack(latents, cotangent, chunk, after=()):
    _, frames, positions, width = latents.shape
    steps = 2
    ranks = positions // 8
    spec = pl.BlockSpec((1, frames, positions // steps, width), lambda i: (0, 0, i, 0))
    return pl.pallas_call(
        functools.partial(pack_kernel, chunk),
        grid=(steps,),
        in_specs=[spec, spec] + [pl.BlockSpec(memory_space=pl.ANY)] * len(after),
        out_specs=pl.BlockSpec((ranks // steps, ROWS_IN, width), lambda i: (i, 0, 0)),
        out_shape=jax.ShapeDtypeStruct((ranks, ROWS_IN, width), BF16),
        compiler_params=pltpu.CompilerParams(vmem_limit_bytes=VMEM),
        cost_estimate=pl.CostEstimate(flops=4_000_000, bytes_accessed=3_600_000, transcendentals=0),
        name="pack",
    )(latents, cotangent, *after)


def tie_kernel(value_ref, other_ref, o_ref):
    del value_ref, other_ref, o_ref


def tie(value, other):
    any_space = pl.BlockSpec(memory_space=pl.ANY)
    return pl.pallas_call(
        tie_kernel,
        in_specs=[any_space, any_space],
        out_specs=any_space,
        out_shape=jax.ShapeDtypeStruct(value.shape, value.dtype),
        input_output_aliases={0: 0},
        name="tie",
    )(value, other)


def unpack_kernel(first_ref, second_ref, block_ref, grad_ref):
    ranks = first_ref.shape[0]
    for c in range(TILES):
        cols = slice(LANES * c, LANES * (c + 1))
        first, second = first_ref[:, :, cols].astype(F32), second_ref[:, :, cols].astype(F32)
        for at, ref in ((0, block_ref), (8, grad_ref)):
            for i in range(2):
                tile = trade(first[:, at : at + 8], second[:, at : at + 8], i)
                ref[0, i, :, cols] = tile.reshape(ranks * 8, LANES).astype(BF16)


def unpack(first, second, shape):
    _, frames, positions, width = shape
    steps = 2
    spec = pl.BlockSpec((1, frames, positions // steps, width), lambda i: (0, 0, i, 0))
    out = jax.ShapeDtypeStruct(shape, BF16)
    return pl.pallas_call(
        unpack_kernel,
        grid=(steps,),
        in_specs=[
            pl.BlockSpec((x.shape[0] // steps, ROWS_IN, width), lambda i: (i, 0, 0))
            for x in (first, second)
        ],
        out_specs=[spec, spec],
        out_shape=[out, out],
        compiler_params=pltpu.CompilerParams(vmem_limit_bytes=VMEM),
        cost_estimate=pl.CostEstimate(flops=4_000_000, bytes_accessed=5_000_000, transcendentals=0),
        name="unpack",
    )(first, second)


def init_segments(seg, spread, fold):
    r, c = iota((D, REST), 0), iota((D, REST), 1)
    head = jnp.where(r < MAIN, r >> 6, (r - MAIN) >> 3)
    seg[...] = one_hot(head == (c >> 3))
    entry = jnp.where(r < MAIN, r & 63, 64 + (r & 7))
    fold[...] = one_hot(entry == c)
    r, c = iota((2 * REST, MAIN), 0), iota((2 * REST, MAIN), 1)
    spread[...] = one_hot((r & (REST - 1)) == 8 * (c >> 6))


def terms(value):
    high = value.astype(BF16)
    left = value - high.astype(F32)
    mid = left.astype(BF16)
    return high, mid, (left - mid.astype(F32)).astype(BF16)


def both(per_head):
    high = per_head.astype(BF16)
    return jnp.concatenate([high, (per_head - high.astype(F32)).astype(BF16)], 1)


def head_masks(t):
    c = iota((1, 256), 1)
    head = jnp.where(c < 128, (c >> 6) + 2 * t, (c - 128) >> 3)
    return [one_hot(head == h) for h in (2 * t, 2 * t + 1)]


def unit_of(ref, rows, t):
    return jnp.concatenate([ref[rows, 128 * t : 128 * (t + 1)], ref[rows, MAIN:]], 1)


def stacked(block, masks):
    return [
        jnp.concatenate([block[:FR] * masks[0], block[:FR] * masks[1]], 0),
        jnp.concatenate([block[FR:] * masks[0], block[FR:] * masks[1]], 0),
    ]


def diagonal(block):
    zero = jnp.zeros((FR, 256), BF16)
    return jnp.concatenate(
        [
            jnp.concatenate([block[:FR], zero], 1),
            jnp.concatenate([zero, block[FR:]], 1),
        ],
        0,
    )


def by_position(block):
    lane, zero = iota((128, 128), 1), jnp.zeros((128, 128), F32)
    own = lane < FR
    return jnp.concatenate(
        [jnp.where(own, block, zero), jnp.where(own, zero, block)], 0
    ).astype(BF16)


def own_rows(product, masks):
    zero, one = masks[0].astype(F32), masks[1].astype(F32)
    return jnp.concatenate(
        [
            product[:64] * zero + product[64:128] * one,
            product[128:192] * zero + product[192:] * one,
        ],
        0,
    )


def loop(count, body):
    def step(i, _):
        body(i)
        return 0

    lax.fori_loop(0, count, step, 0)


def over_columns(total, body):
    for b in range(0, total, BLOCK):
        body(slice(b, min(b + BLOCK, total)))


def over_rows(size, body):
    for i in range(0, TOK, size):
        body(slice(i, i + size))


def lane_tiles():
    return [slice(LANES * c, LANES * (c + 1)) for c in range(TILES)]


def sub_block(
    last,
    count_ref,
    in_hbm,
    table_hbm,
    clip_hbm,
    q_gain_hbm,
    k_gain_hbm,
    wqkv_hbm,
    wout_hbm,
    before_hbm,
    out_hbm,
    sums,
    out_ref,
    table_ref,
    clip_ref,
    q_gain_ref,
    k_gain_ref,
    before_ref,
    in_ref,
    wqkv,
    wout,
    sems,
    frames,
    xp,
    unit,
    istd,
    cp,
    gy,
    normed,
    proj,
    gatt,
    qn,
    kn,
    vn,
    rq,
    rk,
    dq,
    dk,
    dqkv,
    seg,
    spread,
    fold,
    bias,
    mod_ref,
    gain_ref,
):
    ranks = in_ref.shape[0]
    att, gn = gy, normed
    load_qkv = pltpu.make_async_copy(wqkv_hbm, wqkv, sems.at[0])
    load_out = pltpu.make_async_copy(wout_hbm, wout, sems.at[1])
    load_in = pltpu.make_async_copy(in_hbm, in_ref, sems.at[2])
    small = [
        pltpu.make_async_copy(source, target, sems.at[3 + i])
        for i, (source, target) in enumerate(
            (
                (table_hbm, table_ref),
                (clip_hbm, clip_ref),
                (q_gain_hbm, q_gain_ref),
                (k_gain_hbm, k_gain_ref),
                (before_hbm, before_ref),
            )
        )
    ]
    load_in.start()
    for copy in small:
        copy.start()
    load_out.start()
    load_qkv.start()
    init_segments(seg, spread, fold)
    key = iota((128, 128), 0) & (FR - 1)
    valid = 2 * (key & 31) + (key >> 5) < count_ref[0]
    bias[...] = jnp.where(valid, jnp.float32(0), jnp.float32(-1e30))
    for copy in small:
        copy.wait()
    sums[...] = before_ref[...]
    mod_ref[...] = table_ref[...] + clip_ref[...]
    for part, ref in enumerate((q_gain_ref, k_gain_ref)):
        gain_ref[part : part + 1, :] = sum(dot(x, fold[:, :HEAD], NT) for x in terms(ref[...]))

    def strided(p, first, own):
        return pl.ds(first + own * POS + p, ranks, stride=ROWS_IN)

    def gather(c, p, first):
        return jnp.concatenate([frames[c, strided(p, first, own), :] for own in range(2)], 0)

    def scatter(c, p, first, value):
        for own in range(2):
            frames[c, strided(p, first, own), :] = value[own * ranks : (own + 1) * ranks]

    def position_rows(p):
        if isinstance(p, int):
            return slice(p * FR, (p + 1) * FR)
        return pl.ds(pl.multiple_of(p * FR, FR), FR)

    load_in.wait()
    for c, cols in enumerate(lane_tiles()):
        frames[c] = in_ref[:, :, cols].reshape(ranks * ROWS_IN, LANES).astype(F32)

    def arrive(p):
        rows = position_rows(p)
        for c, cols in enumerate(lane_tiles()):
            cot = gather(c, p, 8)
            cp[rows, cols] = cot
            gy[rows, cols] = (cot * mod_ref[2:3, cols]).astype(BF16)

    def norm(p):
        rows = position_rows(p)
        parts = [gather(c, p, 0) for c in range(TILES)]
        mean = jnp.sum(sum(parts), -1, keepdims=True) * (1.0 / D)
        centred = [x - mean for x in parts]
        square = jnp.sum(sum(x * x for x in centred), -1, keepdims=True) * (1.0 / D)
        inv = lax.rsqrt(square + EPS)
        istd[rows, :] = jnp.broadcast_to(inv, (FR, LANES))
        for c, cols in enumerate(lane_tiles()):
            xp[rows, cols] = parts[c]
            u = centred[c] * inv
            unit[rows, cols] = u
            normed[rows, cols] = (u * (1.0 + mod_ref[1:2, cols]) + mod_ref[0:1, cols]).astype(BF16)

    loop(POS, arrive)

    def grad_attention(cols):
        gatt[:, cols] = dot(gy[...], wout[cols, :], NT).astype(BF16)

    load_out.wait()
    norm(0)
    grad_attention(slice(0, BLOCK))
    norm(1)
    grad_attention(slice(BLOCK, 2 * BLOCK))
    norm(2)
    grad_attention(slice(2 * BLOCK, D))
    norm(3)

    def project(cols):
        proj[:, cols] = dot(normed[...], wqkv[:, cols])

    load_qkv.wait()
    over_columns(QK, project)

    def project_values(cols):
        vn[:, cols] = dot(normed[...], wqkv[:, QK + cols.start : QK + cols.stop]).astype(BF16)


    def heads(part, n_ref, r_ref, rows):
        main = slice(MAIN_AT[part], MAIN_AT[part] + MAIN)
        rest = slice(REST_AT[part], REST_AT[part] + REST)
        m, t = proj[rows, main], proj[rows, rest]
        total = sum(dot(part, seg[:MAIN, :]) for part in terms(m * m)[:2])
        total = total + sum(dot(part, seg[MAIN:, :]) for part in terms(t * t)[:2])
        inv = lax.rsqrt(total * (1.0 / HEAD) + EPS)
        r_ref[rows, :] = inv
        pair = both(inv)
        for b in range(0, MAIN, 256):
            cols = slice(MAIN_AT[part] + b, MAIN_AT[part] + b + 256)
            hat = proj[rows, cols] * dot(pair, spread[:, b : b + 256])
            proj[rows, cols] = hat
            n_ref[rows, b : b + 256] = (hat * gain_ref[part : part + 1, b : b + 256]).astype(BF16)
        hat = t * inv
        proj[rows, rest] = hat
        n_ref[rows, MAIN:] = (hat * gain_ref[part : part + 1, MAIN:]).astype(BF16)


    everything = slice(0, TOK)
    project_values(slice(0, BLOCK))
    heads(0, qn, rq, everything)
    project_values(slice(BLOCK, 2 * BLOCK))
    heads(1, kn, rk, everything)
    project_values(slice(2 * BLOCK, D))

    def attend(rows):
        rest = [jnp.zeros((ROWS, REST), F32)] * 4
        ops, soft = [], []
        for t in range(HEADS // 2):
            masks = head_masks(t)
            keys = stacked(unit_of(kn, rows, t), masks)
            vals = stacked(unit_of(vn, rows, t), masks)
            query = diagonal(unit_of(qn, rows, t))
            grad = diagonal(unit_of(gatt, rows, t))
            s = dot(jnp.concatenate(keys, 1), query, NT) * (HEAD**-0.5) + bias[...]
            dp = dot(jnp.concatenate(vals, 1), grad, NT)
            ops.append((t, masks, keys, vals, s, dp))
        for *_, s, dp in ops:
            s, dp = s.reshape(2, FR, 128), dp.reshape(2, FR, 128)
            e = jnp.exp(s - jnp.max(s, 1, keepdims=True))
            prob = e * (1.0 / jnp.sum(e, 1, keepdims=True))
            delta = jnp.sum(prob * dp, 1, keepdims=True)
            ds = (prob * (dp - delta) * (HEAD**-0.5)).reshape(128, 128)
            prob = prob.reshape(128, 128)
            soft.append((prob, ds))
        for (t, masks, keys, vals, _, _), (prob, ds) in zip(ops, soft):
            pt, dt = prob.T.astype(BF16), ds.T.astype(BF16)
            cols = slice(128 * t, 128 * (t + 1))
            out = jnp.concatenate([dot(pt[:FR], vals[0]), dot(pt[FR:], vals[1])], 0)
            gq = jnp.concatenate([dot(dt[:FR], keys[0]), dot(dt[FR:], keys[1])], 0)
            gk = own_rows(dot(by_position(ds), unit_of(qn, rows, t)), masks)
            gv = own_rows(dot(by_position(prob), unit_of(gatt, rows, t)), masks)
            att[rows, cols] = out[:, :128].astype(BF16)
            dq[rows, cols] = gq[:, :128].astype(BF16)
            dk[rows, cols] = gk[:, :128].astype(BF16)
            dqkv[rows, QK + 128 * t : QK + 128 * (t + 1)] = gv[:, :128].astype(BF16)
            rest = [a + b[:, 128:] for a, b in zip(rest, (out, gq, gk, gv))]
        att[rows, MAIN:] = rest[0].astype(BF16)
        dq[rows, MAIN:] = rest[1].astype(BF16)
        dk[rows, MAIN:] = rest[2].astype(BF16)
        dqkv[rows, QK + MAIN :] = rest[3].astype(BF16)

    over_rows(ROWS, attend)

    def out_project(first, size):
        cols = slice(first, first + size)
        y = dot(att[...], wout[:, cols])
        sums[2:3, cols] += jnp.sum(cp[:, cols] * y, 0, keepdims=True)
        value = xp[:, cols] + mod_ref[2:3, cols] * y
        for c in range(size // LANES):
            for p in range(POS):
                tile = value[p * FR : (p + 1) * FR, c * LANES : (c + 1) * LANES]
                scatter(first // LANES + c, p, 0, tile)


    def heads_grad(part, d_ref, r_ref, rows):
        main = slice(MAIN_AT[part], MAIN_AT[part] + MAIN)
        rest = slice(REST_AT[part], REST_AT[part] + REST)
        gain = gain_ref[part : part + 1, :]
        row = slice(3 + part, 4 + part)
        um, ur = d_ref[rows, :MAIN].astype(F32), d_ref[rows, MAIN:].astype(F32)
        wm, wr = um * proj[rows, main], ur * proj[rows, rest]
        sums[row, :MAIN] += jnp.sum(wm, 0, keepdims=True)
        sums[row, MAIN:] += jnp.sum(wr, 0, keepdims=True)
        total = dot((wm * gain[:, :MAIN]).astype(BF16), seg[:MAIN, :]) + dot(
            (wr * gain[:, MAIN:]).astype(BF16), seg[MAIN:, :]
        )
        inner = total * (1.0 / HEAD)
        inv = r_ref[rows, :]
        pair, inner_pair = both(inv), both(inner)
        for b in range(0, MAIN, 256):
            cols = slice(MAIN_AT[part] + b, MAIN_AT[part] + b + 256)
            a = d_ref[rows, b : b + 256].astype(F32) * gain[:, b : b + 256]
            picked = spread[:, b : b + 256]
            value = dot(pair, picked) * (a - proj[rows, cols] * dot(inner_pair, picked))
            dqkv[rows, cols] = value.astype(BF16)
        value = inv * (ur * gain[:, MAIN:] - proj[rows, rest] * inner)
        dqkv[rows, rest] = value.astype(BF16)


    out_project(0, BLOCK)
    heads_grad(0, dq, rq, everything)
    out_project(BLOCK, BLOCK)
    heads_grad(1, dk, rk, everything)
    out_project(2 * BLOCK, D - 2 * BLOCK)

    def grad_normed(cols):
        gn[:, cols] = dot(dqkv[...], wqkv[cols, :], NT).astype(BF16)

    over_columns(D, grad_normed)

    def layer(p):
        rows = position_rows(p)
        grads = [gn[rows, cols].astype(F32) for cols in lane_tiles()]
        units = [unit[rows, cols] for cols in lane_tiles()]
        scaled = []
        for g, u, cols in zip(grads, units, lane_tiles()):
            sums[0:1, cols] += jnp.sum(g, 0, keepdims=True)
            sums[1:2, cols] += jnp.sum(g * u, 0, keepdims=True)
            scaled.append(g * (1.0 + mod_ref[1:2, cols]))
        first = jnp.sum(sum(scaled), -1, keepdims=True) * (1.0 / D)
        second = jnp.sum(sum(g * u for g, u in zip(scaled, units)), -1, keepdims=True) * (1.0 / D)
        inv = istd[rows, :]
        for c, cols in enumerate(lane_tiles()):
            value = cp[rows, cols] + inv * (scaled[c] - first - units[c] * second)
            scatter(c, p, 8, value)

    for p in range(POS):
        layer(p)

    if last:
        total = sums[...]
        folded = sum(dot(part, fold[...]) for part in terms(total))
        gains = jnp.concatenate([folded[3:4], folded[4:5], jnp.zeros((1, D - 256), F32)], 1)
        high, low, _ = terms(jnp.concatenate([total[:3], gains], 0))
        sent = jnp.concatenate([high.astype(F32), low.astype(F32)], 0)
    for c, cols in enumerate(lane_tiles()):
        block = frames[c].reshape(ranks, ROWS_IN, LANES)
        if last:
            rows = jnp.broadcast_to(sent[None, :, cols], (ranks, SUMS, LANES))
            block = jnp.concatenate([block, rows], 1)
        out_ref[:, :, cols] = block.astype(BF16)
    leave = pltpu.make_async_copy(out_ref, out_hbm, sems.at[8])
    leave.start()
    leave.wait()


def run_sub_block(last, frame_counts, arrived, modulation, gains, weights, before):
    ranks = arrived.shape[0]
    tok = (TOK, D)
    any_space = pl.BlockSpec(memory_space=pl.ANY)
    vmem = pl.BlockSpec(memory_space=pltpu.VMEM)
    sent = ROWS_IN + SUMS if last else ROWS_IN
    scratch = [
        pltpu.VMEM((ranks, sent, D), BF16),
        pltpu.VMEM((3, D), F32),
        pltpu.VMEM((3, D), F32),
        pltpu.VMEM((1, HEAD), F32),
        pltpu.VMEM((1, HEAD), F32),
        pltpu.VMEM((8, D), F32),
        pltpu.VMEM((ranks, ROWS_IN, D), BF16),
        pltpu.VMEM((D, 3 * D), BF16),
        pltpu.VMEM((D, D), BF16),
        pltpu.SemaphoreType.DMA((9,)),
        pltpu.VMEM((TILES, ranks * ROWS_IN, LANES), F32),
        pltpu.VMEM(tok, F32),
        pltpu.VMEM(tok, F32),
        pltpu.VMEM((TOK, LANES), F32),
        pltpu.VMEM(tok, F32),
        pltpu.VMEM(tok, BF16),
        pltpu.VMEM(tok, BF16),
        pltpu.VMEM((TOK, QK), F32),
        pltpu.VMEM(tok, BF16),
        pltpu.VMEM(tok, BF16),
        pltpu.VMEM(tok, BF16),
        pltpu.VMEM(tok, BF16),
        pltpu.VMEM((TOK, REST), F32),
        pltpu.VMEM((TOK, REST), F32),
        pltpu.VMEM(tok, BF16),
        pltpu.VMEM(tok, BF16),
        pltpu.VMEM((TOK, 3 * D), BF16),
        pltpu.VMEM((D, REST), BF16),
        pltpu.VMEM((2 * REST, MAIN), BF16),
        pltpu.VMEM((D, REST), BF16),
        pltpu.VMEM((128, 128), F32),
        pltpu.VMEM((3, D), F32),
        pltpu.VMEM((2, D), F32),
    ]
    return pl.pallas_call(
        functools.partial(sub_block, last),
        in_specs=[pl.BlockSpec(memory_space=pltpu.SMEM)]
        + [any_space] * 8,
        out_specs=[any_space, vmem],
        out_shape=[
            jax.ShapeDtypeStruct((ranks, sent, D), BF16),
            jax.ShapeDtypeStruct((8, D), F32),
        ],
        scratch_shapes=scratch,
        compiler_params=pltpu.CompilerParams(vmem_limit_bytes=VMEM),
        cost_estimate=pl.CostEstimate(
            flops=12_000_000_000, bytes_accessed=20_000_000, transcendentals=0
        ),
        name="sub_block",
    )(frame_counts, arrived, *modulation, *gains, *weights, before)


def sum_clips(value):
    clips = lax.axis_size("dp")
    one, two, three = (
        lax.ppermute(value, "dp", [(i, i ^ step) for i in range(clips)]) for step in (1, 2, 3)
    )
    return (value + one) + (two + three)


def shards(latents, frame_counts, mod_table, clip_mod, q_gain, k_gain, w_qkv, w_out, cotangent):
    ranks = lax.axis_size("seq")
    modulation = (mod_table, clip_mod[0])
    gains = (q_gain[None], k_gain[None])

    def exchange(rows):
        return lax.all_to_all(rows, "seq", split_axis=0, concat_axis=0, tiled=True)

    weights = split_weights(w_qkv, w_out)
    arrived = [
        exchange(pack(latents, cotangent, 0)),
        exchange(pack(latents, cotangent, 1, after=weights[1:])),
    ]
    sums = jnp.zeros((8, D), F32)
    back = []
    for i in range(CHUNKS):
        last = i == CHUNKS - 1
        out, sums = run_sub_block(last, frame_counts, arrived[i], modulation, gains, weights, sums)
        back.append(exchange(tie(out, back[0]) if last else out))
    pieces = jnp.sum(back[-1][:, ROWS_IN:, :].astype(F32), 0)
    clip_total = pieces[0:4] + pieces[4:8]
    total = sum_clips(clip_total)
    block_out, input_grad = unpack(*back, latents.shape)
    return (
        block_out,
        input_grad,
        clip_total[None, :3],
        total[:3],
        total[3, :HEAD],
        total[3, 128 : 128 + HEAD],
    )


def solution(mesh):
    return jax.shard_map(
        shards,
        mesh=mesh,
        in_specs=(
            P("dp", "seq", None, None),
            P("dp"),
            P(),
            P("dp", None, None),
            P(),
            P(),
            P(),
            P(),
            P("dp", "seq", None, None),
        ),
        out_specs=(
            P("dp", "seq", None, None),
            P("dp", "seq", None, None),
            P("dp", None, None),
            P(),
            P(),
            P(),
        ),
        check_vma=False,
    )
```

```python
import functools

import jax
import jax.numpy as jnp
from jax import lax
from jax.experimental import pallas as pl
from jax.experimental.pallas import tpu as pltpu
from jax.sharding import PartitionSpec as P

EPS = 1e-06
F32 = jnp.float32
BF16 = jnp.bfloat16
HEAD = 72
HEADS = 16
D = HEAD * HEADS
MAIN = 64 * HEADS
REST = 8 * HEADS
QK = 2 * D
MAIN_AT = (0, MAIN, QK)
REST_AT = (2 * MAIN, 2 * MAIN + REST, QK + MAIN)
CHUNKS = 2
POS = 4
FR = 64
TOK = POS * FR
ROWS = 128
PAIRS = TOK // ROWS
BLOCK = 512
LANES = 128
TILES = D // LANES
ROWS_IN = 16
SUMS = 8
MIB = 1024 * 1024
NN = (((1,), (0,)), ((), ()))
NT = (((1,), (1,)), ((), ()))
TN = (((0,), (0,)), ((), ()))


def dot(a, b, dims=NN):
    return lax.dot_general(a, b, dims, preferred_element_type=F32)


def iota(shape, dim):
    return lax.broadcasted_iota(jnp.int32, shape, dim)


def one_hot(cond):
    return jnp.where(cond, jnp.float32(1), jnp.float32(0)).astype(BF16)


def source_main(col):
    return col + 8 * (col >> 6)


def source_rest(col):
    return col + 64 + 64 * (col >> 3)


def window(j):
    return 288 * j // 128 * 128


def split_weights_kernel(qkv_ref, out_ref, qkv_o, out_o, pick, pick_rest):
    @pl.when(pl.program_id(0) == 0)
    def _():
        for j in range(4):
            r, c = iota((384, 256), 0), iota((384, 256), 1)
            pick[j] = one_hot(source_main(c + 256 * j) == r + window(j))
        r, c = iota((D, REST), 0), iota((D, REST), 1)
        pick_rest[...] = one_hot(source_rest(c) == r)

    for part in range(3):
        base = part * D
        for j in range(4):
            lo = base + window(j)
            qkv_o[:, MAIN_AT[part] + 256 * j : MAIN_AT[part] + 256 * (j + 1)] = dot(
                qkv_ref[:, lo : lo + 384], pick[j]
            ).astype(BF16)
        qkv_o[:, REST_AT[part] : REST_AT[part] + REST] = dot(
            qkv_ref[:, base : base + D], pick_rest[...]
        ).astype(BF16)

    for j in range(4):
        out_o[256 * j : 256 * (j + 1), :] = dot(
            pick[j], out_ref[window(j) : window(j) + 384, :], TN
        ).astype(BF16)
    out_o[MAIN:, :] = dot(pick_rest[...], out_ref[...], TN).astype(BF16)


def split_weights(w_qkv, w_out):
    steps = 3
    part = D // steps
    return pl.pallas_call(
        split_weights_kernel,
        grid=(steps,),
        in_specs=[
            pl.BlockSpec((part, 3 * D), lambda i: (i, 0)),
            pl.BlockSpec((D, part), lambda i: (0, i)),
        ],
        out_specs=[
            pl.BlockSpec((part, 3 * D), lambda i: (i, 0)),
            pl.BlockSpec((D, part), lambda i: (0, i)),
        ],
        out_shape=[
            jax.ShapeDtypeStruct((D, 3 * D), BF16),
            jax.ShapeDtypeStruct((D, D), BF16),
        ],
        scratch_shapes=[pltpu.VMEM((4, 384, 256), BF16), pltpu.VMEM((D, REST), BF16)],
        compiler_params=pltpu.CompilerParams(vmem_limit_bytes=60 * MIB),
        cost_estimate=pl.CostEstimate(
            flops=2 * D * D * 1600, bytes_accessed=16 * D * D, transcendentals=0
        ),
        name="split_weights",
    )(w_qkv, w_out)


def trade(first, second, chunk):
    upper = iota(first.shape, 1) < POS
    if chunk == 0:
        return jnp.where(upper, first, pltpu.roll(second, POS, 1))
    return jnp.where(upper, pltpu.roll(first, POS, 1), second)


def pack_kernel(chunk, lat_ref, cot_ref, *refs):
    o_ref = refs[-1]
    ranks, _, width = o_ref.shape
    for c in range(TILES):
        cols = slice(LANES * c, LANES * (c + 1))
        halves = []
        for ref in (lat_ref, cot_ref):
            tiles = [ref[0, i, :, cols].astype(F32).reshape(ranks, 8, LANES) for i in range(2)]
            halves.append(trade(*tiles, chunk))
        o_ref[:, :, cols] = jnp.concatenate(halves, 1).astype(BF16)


def pack(latents, cotangent, chunk, after=()):
    _, frames, positions, width = latents.shape
    steps = 2
    ranks = positions // 8
    spec = pl.BlockSpec((1, frames, positions // steps, width), lambda i: (0, 0, i, 0))
    return pl.pallas_call(
        functools.partial(pack_kernel, chunk),
        grid=(steps,),
        in_specs=[spec, spec] + [pl.BlockSpec(memory_space=pl.ANY)] * len(after),
        out_specs=pl.BlockSpec((ranks // steps, ROWS_IN, width), lambda i: (i, 0, 0)),
        out_shape=jax.ShapeDtypeStruct((ranks, ROWS_IN, width), BF16),
        compiler_params=pltpu.CompilerParams(vmem_limit_bytes=60 * MIB),
        cost_estimate=pl.CostEstimate(flops=4_000_000, bytes_accessed=3_600_000, transcendentals=0),
        name="pack",
    )(latents, cotangent, *after)


def tie_kernel(value_ref, other_ref, o_ref):
    del value_ref, other_ref, o_ref


def tie(value, other):
    any_space = pl.BlockSpec(memory_space=pl.ANY)
    return pl.pallas_call(
        tie_kernel,
        in_specs=[any_space, any_space],
        out_specs=any_space,
        out_shape=jax.ShapeDtypeStruct(value.shape, value.dtype),
        input_output_aliases={0: 0},
        compiler_params=pltpu.CompilerParams(vmem_limit_bytes=MIB),
        name="tie",
    )(value, other)


def unpack_kernel(first_ref, second_ref, block_ref, grad_ref):
    ranks = first_ref.shape[0]
    for c in range(TILES):
        cols = slice(LANES * c, LANES * (c + 1))
        first, second = first_ref[:, :, cols].astype(F32), second_ref[:, :, cols].astype(F32)
        for at, ref in ((0, block_ref), (8, grad_ref)):
            for i in range(2):
                tile = trade(first[:, at : at + 8], second[:, at : at + 8], i)
                ref[0, i, :, cols] = tile.reshape(ranks * 8, LANES).astype(BF16)


def unpack(first, second, shape):
    _, frames, positions, width = shape
    steps = 2
    spec = pl.BlockSpec((1, frames, positions // steps, width), lambda i: (0, 0, i, 0))
    out = jax.ShapeDtypeStruct(shape, BF16)
    return pl.pallas_call(
        unpack_kernel,
        grid=(steps,),
        in_specs=[
            pl.BlockSpec((x.shape[0] // steps, ROWS_IN, width), lambda i: (i, 0, 0))
            for x in (first, second)
        ],
        out_specs=[spec, spec],
        out_shape=[out, out],
        compiler_params=pltpu.CompilerParams(vmem_limit_bytes=50 * MIB),
        cost_estimate=pl.CostEstimate(flops=4_000_000, bytes_accessed=5_000_000, transcendentals=0),
        name="unpack",
    )(first, second)


def init_segments(seg, spread, fold):
    r, c = iota((D, REST), 0), iota((D, REST), 1)
    head = jnp.where(r < MAIN, r >> 6, (r - MAIN) >> 3)
    seg[...] = one_hot(head == (c >> 3))
    entry = jnp.where(r < MAIN, r & 63, 64 + (r & 7))
    fold[...] = one_hot(entry == c)
    r, c = iota((2 * REST, MAIN), 0), iota((2 * REST, MAIN), 1)
    spread[...] = one_hot((r & (REST - 1)) == 8 * (c >> 6))


def terms(value):
    high = value.astype(BF16)
    left = value - high.astype(F32)
    mid = left.astype(BF16)
    return high, mid, (left - mid.astype(F32)).astype(BF16)


def both(per_head):
    high = per_head.astype(BF16)
    return jnp.concatenate([high, (per_head - high.astype(F32)).astype(BF16)], 1)


def head_masks(t):
    c = iota((1, 256), 1)
    head = jnp.where(c < 128, (c >> 6) + 2 * t, (c - 128) >> 3)
    return [one_hot(head == h) for h in (2 * t, 2 * t + 1)]


def unit_of(ref, rows, t):
    return jnp.concatenate([ref[rows, 128 * t : 128 * (t + 1)], ref[rows, MAIN:]], 1)


def stacked(block, masks):
    return [
        jnp.concatenate([block[:FR] * masks[0], block[:FR] * masks[1]], 0),
        jnp.concatenate([block[FR:] * masks[0], block[FR:] * masks[1]], 0),
    ]


def diagonal(block):
    zero = jnp.zeros((FR, 256), BF16)
    return jnp.concatenate(
        [
            jnp.concatenate([block[:FR], zero], 1),
            jnp.concatenate([zero, block[FR:]], 1),
        ],
        0,
    )


def by_position(block):
    lane, zero = iota((128, 128), 1), jnp.zeros((128, 128), F32)
    own = lane < FR
    return jnp.concatenate(
        [jnp.where(own, block, zero), jnp.where(own, zero, block)], 0
    ).astype(BF16)


def own_rows(product, masks):
    zero, one = masks[0].astype(F32), masks[1].astype(F32)
    return jnp.concatenate(
        [
            product[:64] * zero + product[64:128] * one,
            product[128:192] * zero + product[192:] * one,
        ],
        0,
    )


def loop(count, body):
    def step(i, _):
        body(i)
        return 0

    lax.fori_loop(0, count, step, 0)


def over_columns(total, body):
    for b in range(0, total, BLOCK):
        body(slice(b, min(b + BLOCK, total)))


def over_rows(size, body):
    for i in range(0, TOK, size):
        body(slice(i, i + size))


def lane_tiles():
    return [slice(LANES * c, LANES * (c + 1)) for c in range(TILES)]


def sub_block(
    last,
    count_ref,
    in_hbm,
    table_hbm,
    clip_hbm,
    q_gain_hbm,
    k_gain_hbm,
    wqkv_hbm,
    wout_hbm,
    before_hbm,
    out_ref,
    sums,
    table_ref,
    clip_ref,
    q_gain_ref,
    k_gain_ref,
    before_ref,
    in_ref,
    wqkv,
    wout,
    sems,
    frames,
    xp,
    unit,
    istd,
    cp,
    gy,
    normed,
    proj,
    gatt,
    qn,
    kn,
    vn,
    rq,
    rk,
    dq,
    dk,
    dqkv,
    seg,
    spread,
    fold,
    bias,
    mod_ref,
    gain_ref,
):
    ranks = in_ref.shape[0]
    att, gn = gy, normed
    load_qkv = pltpu.make_async_copy(wqkv_hbm, wqkv, sems.at[0])
    load_out = pltpu.make_async_copy(wout_hbm, wout, sems.at[1])
    load_in = pltpu.make_async_copy(in_hbm, in_ref, sems.at[2])
    small = [
        pltpu.make_async_copy(source, target, sems.at[3 + i])
        for i, (source, target) in enumerate(
            (
                (table_hbm, table_ref),
                (clip_hbm, clip_ref),
                (q_gain_hbm, q_gain_ref),
                (k_gain_hbm, k_gain_ref),
                (before_hbm, before_ref),
            )
        )
    ]
    load_in.start()
    for copy in small:
        copy.start()
    load_out.start()
    load_qkv.start()
    init_segments(seg, spread, fold)
    key = iota((128, 128), 0) & (FR - 1)
    valid = 2 * (key & 31) + (key >> 5) < count_ref[0]
    bias[...] = jnp.where(valid, jnp.float32(0), jnp.float32(-1e30))
    for copy in small:
        copy.wait()
    sums[...] = before_ref[...]
    mod_ref[...] = table_ref[...] + clip_ref[...]
    for part, ref in enumerate((q_gain_ref, k_gain_ref)):
        gain_ref[part : part + 1, :] = sum(dot(x, fold[:, :HEAD], NT) for x in terms(ref[...]))

    def strided(p, first, own):
        return pl.ds(first + own * POS + p, ranks, stride=ROWS_IN)

    def gather(c, p, first):
        return jnp.concatenate([frames[c, strided(p, first, own), :] for own in range(2)], 0)

    def scatter(c, p, first, value):
        for own in range(2):
            frames[c, strided(p, first, own), :] = value[own * ranks : (own + 1) * ranks]

    def position_rows(p):
        if isinstance(p, int):
            return slice(p * FR, (p + 1) * FR)
        return pl.ds(pl.multiple_of(p * FR, FR), FR)

    load_in.wait()
    for c, cols in enumerate(lane_tiles()):
        frames[c] = in_ref[:, :, cols].reshape(ranks * ROWS_IN, LANES).astype(F32)

    def arrive(p):
        rows = position_rows(p)
        for c, cols in enumerate(lane_tiles()):
            cot = gather(c, p, 8)
            cp[rows, cols] = cot
            gy[rows, cols] = (cot * mod_ref[2:3, cols]).astype(BF16)

    def norm(p):
        rows = position_rows(p)
        parts = [gather(c, p, 0) for c in range(TILES)]
        mean = jnp.sum(sum(parts), -1, keepdims=True) * (1.0 / D)
        centred = [x - mean for x in parts]
        square = jnp.sum(sum(x * x for x in centred), -1, keepdims=True) * (1.0 / D)
        inv = lax.rsqrt(square + EPS)
        istd[rows, :] = jnp.broadcast_to(inv, (FR, LANES))
        for c, cols in enumerate(lane_tiles()):
            xp[rows, cols] = parts[c]
            u = centred[c] * inv
            unit[rows, cols] = u
            normed[rows, cols] = (u * (1.0 + mod_ref[1:2, cols]) + mod_ref[0:1, cols]).astype(BF16)

    loop(POS, arrive)

    def grad_attention(cols):
        gatt[:, cols] = dot(gy[...], wout[cols, :], NT).astype(BF16)

    load_out.wait()
    norm(0)
    grad_attention(slice(0, BLOCK))
    norm(1)
    grad_attention(slice(BLOCK, 2 * BLOCK))
    norm(2)
    grad_attention(slice(2 * BLOCK, D))
    norm(3)

    def project(cols):
        proj[:, cols] = dot(normed[...], wqkv[:, cols])

    load_qkv.wait()
    over_columns(QK, project)

    def project_values(cols):
        vn[:, cols] = dot(normed[...], wqkv[:, QK + cols.start : QK + cols.stop]).astype(BF16)


    def heads(part, n_ref, r_ref, rows):
        main = slice(MAIN_AT[part], MAIN_AT[part] + MAIN)
        rest = slice(REST_AT[part], REST_AT[part] + REST)
        m, t = proj[rows, main], proj[rows, rest]
        total = sum(dot(part, seg[:MAIN, :]) for part in terms(m * m)[:2])
        total = total + sum(dot(part, seg[MAIN:, :]) for part in terms(t * t)[:2])
        inv = lax.rsqrt(total * (1.0 / HEAD) + EPS)
        r_ref[rows, :] = inv
        pair = both(inv)
        for b in range(0, MAIN, 256):
            cols = slice(MAIN_AT[part] + b, MAIN_AT[part] + b + 256)
            hat = proj[rows, cols] * dot(pair, spread[:, b : b + 256])
            proj[rows, cols] = hat
            n_ref[rows, b : b + 256] = (hat * gain_ref[part : part + 1, b : b + 256]).astype(BF16)
        hat = t * inv
        proj[rows, rest] = hat
        n_ref[rows, MAIN:] = (hat * gain_ref[part : part + 1, MAIN:]).astype(BF16)


    everything = slice(0, TOK)
    project_values(slice(0, BLOCK))
    heads(0, qn, rq, everything)
    project_values(slice(BLOCK, 2 * BLOCK))
    heads(1, kn, rk, everything)
    project_values(slice(2 * BLOCK, D))

    def attend(rows):
        rest = [jnp.zeros((ROWS, REST), F32)] * 4
        ops, soft = [], []
        for t in range(HEADS // 2):
            masks = head_masks(t)
            keys = stacked(unit_of(kn, rows, t), masks)
            vals = stacked(unit_of(vn, rows, t), masks)
            query = diagonal(unit_of(qn, rows, t))
            grad = diagonal(unit_of(gatt, rows, t))
            s = dot(jnp.concatenate(keys, 1), query, NT) * (HEAD**-0.5) + bias[...]
            dp = dot(jnp.concatenate(vals, 1), grad, NT)
            ops.append((t, masks, keys, vals, s, dp))
        for *_, s, dp in ops:
            s, dp = s.reshape(2, FR, 128), dp.reshape(2, FR, 128)
            e = jnp.exp(s - jnp.max(s, 1, keepdims=True))
            prob = e * (1.0 / jnp.sum(e, 1, keepdims=True))
            delta = jnp.sum(prob * dp, 1, keepdims=True)
            ds = (prob * (dp - delta) * (HEAD**-0.5)).reshape(128, 128)
            prob = prob.reshape(128, 128)
            soft.append((prob, ds))
        for (t, masks, keys, vals, _, _), (prob, ds) in zip(ops, soft):
            pt, dt = prob.T.astype(BF16), ds.T.astype(BF16)
            cols = slice(128 * t, 128 * (t + 1))
            out = jnp.concatenate([dot(pt[:FR], vals[0]), dot(pt[FR:], vals[1])], 0)
            gq = jnp.concatenate([dot(dt[:FR], keys[0]), dot(dt[FR:], keys[1])], 0)
            gk = own_rows(dot(by_position(ds), unit_of(qn, rows, t)), masks)
            gv = own_rows(dot(by_position(prob), unit_of(gatt, rows, t)), masks)
            att[rows, cols] = out[:, :128].astype(BF16)
            dq[rows, cols] = gq[:, :128].astype(BF16)
            dk[rows, cols] = gk[:, :128].astype(BF16)
            dqkv[rows, QK + 128 * t : QK + 128 * (t + 1)] = gv[:, :128].astype(BF16)
            rest = [a + b[:, 128:] for a, b in zip(rest, (out, gq, gk, gv))]
        att[rows, MAIN:] = rest[0].astype(BF16)
        dq[rows, MAIN:] = rest[1].astype(BF16)
        dk[rows, MAIN:] = rest[2].astype(BF16)
        dqkv[rows, QK + MAIN :] = rest[3].astype(BF16)

    over_rows(ROWS, attend)

    def out_project(first, size):
        cols = slice(first, first + size)
        y = dot(att[...], wout[:, cols])
        sums[2:3, cols] += jnp.sum(cp[:, cols] * y, 0, keepdims=True)
        value = xp[:, cols] + mod_ref[2:3, cols] * y
        for c in range(size // LANES):
            for p in range(POS):
                tile = value[p * FR : (p + 1) * FR, c * LANES : (c + 1) * LANES]
                scatter(first // LANES + c, p, 0, tile)


    def heads_grad(part, d_ref, r_ref, rows):
        main = slice(MAIN_AT[part], MAIN_AT[part] + MAIN)
        rest = slice(REST_AT[part], REST_AT[part] + REST)
        gain = gain_ref[part : part + 1, :]
        row = slice(3 + part, 4 + part)
        um, ur = d_ref[rows, :MAIN].astype(F32), d_ref[rows, MAIN:].astype(F32)
        wm, wr = um * proj[rows, main], ur * proj[rows, rest]
        sums[row, :MAIN] += jnp.sum(wm, 0, keepdims=True)
        sums[row, MAIN:] += jnp.sum(wr, 0, keepdims=True)
        total = dot((wm * gain[:, :MAIN]).astype(BF16), seg[:MAIN, :]) + dot(
            (wr * gain[:, MAIN:]).astype(BF16), seg[MAIN:, :]
        )
        inner = total * (1.0 / HEAD)
        inv = r_ref[rows, :]
        pair, inner_pair = both(inv), both(inner)
        for b in range(0, MAIN, 256):
            cols = slice(MAIN_AT[part] + b, MAIN_AT[part] + b + 256)
            a = d_ref[rows, b : b + 256].astype(F32) * gain[:, b : b + 256]
            picked = spread[:, b : b + 256]
            value = dot(pair, picked) * (a - proj[rows, cols] * dot(inner_pair, picked))
            dqkv[rows, cols] = value.astype(BF16)
        value = inv * (ur * gain[:, MAIN:] - proj[rows, rest] * inner)
        dqkv[rows, rest] = value.astype(BF16)


    out_project(0, BLOCK)
    heads_grad(0, dq, rq, everything)
    out_project(BLOCK, BLOCK)
    heads_grad(1, dk, rk, everything)
    out_project(2 * BLOCK, D - 2 * BLOCK)

    def grad_normed(cols):
        gn[:, cols] = dot(dqkv[...], wqkv[cols, :], NT).astype(BF16)

    over_columns(D, grad_normed)

    def layer(p):
        rows = position_rows(p)
        grads = [gn[rows, cols].astype(F32) for cols in lane_tiles()]
        units = [unit[rows, cols] for cols in lane_tiles()]
        scaled = []
        for g, u, cols in zip(grads, units, lane_tiles()):
            sums[0:1, cols] += jnp.sum(g, 0, keepdims=True)
            sums[1:2, cols] += jnp.sum(g * u, 0, keepdims=True)
            scaled.append(g * (1.0 + mod_ref[1:2, cols]))
        first = jnp.sum(sum(scaled), -1, keepdims=True) * (1.0 / D)
        second = jnp.sum(sum(g * u for g, u in zip(scaled, units)), -1, keepdims=True) * (1.0 / D)
        inv = istd[rows, :]
        for c, cols in enumerate(lane_tiles()):
            value = cp[rows, cols] + inv * (scaled[c] - first - units[c] * second)
            scatter(c, p, 8, value)

    for p in range(POS):
        layer(p)

    if last:
        total = sums[...]
        folded = sum(dot(part, fold[...]) for part in terms(total))
        gains = jnp.concatenate([folded[3:4], folded[4:5], jnp.zeros((1, D - 256), F32)], 1)
        high, low, _ = terms(jnp.concatenate([total[:3], gains], 0))
        sent = jnp.concatenate([high.astype(F32), low.astype(F32)], 0)
    for c, cols in enumerate(lane_tiles()):
        block = frames[c].reshape(ranks, ROWS_IN, LANES)
        if last:
            rows = jnp.broadcast_to(sent[None, :, cols], (ranks, SUMS, LANES))
            block = jnp.concatenate([block, rows], 1)
        out_ref[:, :, cols] = block.astype(BF16)


def run_sub_block(last, frame_counts, arrived, modulation, gains, weights, before):
    ranks = arrived.shape[0]
    tok = (TOK, D)
    any_space = pl.BlockSpec(memory_space=pl.ANY)
    vmem = pl.BlockSpec(memory_space=pltpu.VMEM)
    sent = ROWS_IN + SUMS if last else ROWS_IN
    scratch = [
        pltpu.VMEM((3, D), F32),
        pltpu.VMEM((3, D), F32),
        pltpu.VMEM((1, HEAD), F32),
        pltpu.VMEM((1, HEAD), F32),
        pltpu.VMEM((8, D), F32),
        pltpu.VMEM((ranks, ROWS_IN, D), BF16),
        pltpu.VMEM((D, 3 * D), BF16),
        pltpu.VMEM((D, D), BF16),
        pltpu.SemaphoreType.DMA((8,)),
        pltpu.VMEM((TILES, ranks * ROWS_IN, LANES), F32),
        pltpu.VMEM(tok, F32),
        pltpu.VMEM(tok, F32),
        pltpu.VMEM((TOK, LANES), F32),
        pltpu.VMEM(tok, F32),
        pltpu.VMEM(tok, BF16),
        pltpu.VMEM(tok, BF16),
        pltpu.VMEM((TOK, QK), F32),
        pltpu.VMEM(tok, BF16),
        pltpu.VMEM(tok, BF16),
        pltpu.VMEM(tok, BF16),
        pltpu.VMEM(tok, BF16),
        pltpu.VMEM((TOK, REST), F32),
        pltpu.VMEM((TOK, REST), F32),
        pltpu.VMEM(tok, BF16),
        pltpu.VMEM(tok, BF16),
        pltpu.VMEM((TOK, 3 * D), BF16),
        pltpu.VMEM((D, REST), BF16),
        pltpu.VMEM((2 * REST, MAIN), BF16),
        pltpu.VMEM((D, REST), BF16),
        pltpu.VMEM((128, 128), F32),
        pltpu.VMEM((3, D), F32),
        pltpu.VMEM((2, D), F32),
    ]
    return pl.pallas_call(
        functools.partial(sub_block, last),
        in_specs=[pl.BlockSpec(memory_space=pltpu.SMEM)]
        + [any_space] * 8,
        out_specs=[vmem, vmem],
        out_shape=[
            jax.ShapeDtypeStruct((ranks, sent, D), BF16),
            jax.ShapeDtypeStruct((8, D), F32),
        ],
        scratch_shapes=scratch,
        compiler_params=pltpu.CompilerParams(vmem_limit_bytes=50 * MIB),
        cost_estimate=pl.CostEstimate(
            flops=12_000_000_000, bytes_accessed=20_000_000, transcendentals=0
        ),
        name="sub_block",
    )(frame_counts, arrived, *modulation, *gains, *weights, before)


def sum_clips(value):
    clips = lax.axis_size("dp")
    one, two, three = (
        lax.ppermute(value, "dp", [(i, i ^ step) for i in range(clips)]) for step in (1, 2, 3)
    )
    return (value + one) + (two + three)


def shards(latents, frame_counts, mod_table, clip_mod, q_gain, k_gain, w_qkv, w_out, cotangent):
    ranks = lax.axis_size("seq")
    modulation = (mod_table, clip_mod[0])
    gains = (q_gain[None], k_gain[None])

    def exchange(rows):
        return lax.all_to_all(rows, "seq", split_axis=0, concat_axis=0, tiled=True)

    weights = split_weights(w_qkv, w_out)
    arrived = [
        exchange(pack(latents, cotangent, 0)),
        exchange(pack(latents, cotangent, 1, after=weights[1:])),
    ]
    sums = jnp.zeros((8, D), F32)
    back = []
    for i in range(CHUNKS):
        last = i == CHUNKS - 1
        out, sums = run_sub_block(last, frame_counts, arrived[i], modulation, gains, weights, sums)
        back.append(exchange(tie(out, back[0]) if last else out))
    pieces = jnp.sum(back[-1][:, ROWS_IN:, :].astype(F32), 0)
    clip_total = pieces[0:4] + pieces[4:8]
    total = sum_clips(clip_total)
    block_out, input_grad = unpack(*back, latents.shape)
    return (
        block_out,
        input_grad,
        clip_total[None, :3],
        total[:3],
        total[3, :HEAD],
        total[3, 128 : 128 + HEAD],
    )


def solution(mesh):
    return jax.shard_map(
        shards,
        mesh=mesh,
        in_specs=(
            P("dp", "seq", None, None),
            P("dp"),
            P(),
            P("dp", None, None),
            P(),
            P(),
            P(),
            P(),
            P("dp", "seq", None, None),
        ),
        out_specs=(
            P("dp", "seq", None, None),
            P("dp", "seq", None, None),
            P("dp", None, None),
            P(),
            P(),
            P(),
        ),
        check_vma=False,
    )
```

```python
import functools

import jax
import jax.numpy as jnp
from jax import lax
from jax.experimental import pallas as pl
from jax.experimental.pallas import tpu as pltpu
from jax.sharding import PartitionSpec as P

EPS = 1e-06
F32 = jnp.float32
BF16 = jnp.bfloat16
HEAD = 72
HEADS = 16
D = HEAD * HEADS
MAIN = 64 * HEADS
REST = 8 * HEADS
QK = 2 * D
MAIN_AT = (0, MAIN, QK)
REST_AT = (2 * MAIN, 2 * MAIN + REST, QK + MAIN)
CHUNKS = 2
POS = 4
FR = 64
TOK = POS * FR
ROWS = 128
PAIRS = TOK // ROWS
BLOCK = 512
LANES = 128
TILES = D // LANES
ROWS_IN = 16
SUMS = 8
MIB = 1024 * 1024
NN = (((1,), (0,)), ((), ()))
NT = (((1,), (1,)), ((), ()))
TN = (((0,), (0,)), ((), ()))


def dot(a, b, dims=NN):
    return lax.dot_general(a, b, dims, preferred_element_type=F32)


def iota(shape, dim):
    return lax.broadcasted_iota(jnp.int32, shape, dim)


def one_hot(cond):
    return jnp.where(cond, jnp.float32(1), jnp.float32(0)).astype(BF16)


def source_main(col):
    return col + 8 * (col >> 6)


def source_rest(col):
    return col + 64 + 64 * (col >> 3)


def window(j):
    return 288 * j // 128 * 128


def split_weights_kernel(qkv_ref, out_ref, qkv_o, out_o, pick, pick_rest):
    @pl.when(pl.program_id(0) == 0)
    def _():
        for j in range(4):
            r, c = iota((384, 256), 0), iota((384, 256), 1)
            pick[j] = one_hot(source_main(c + 256 * j) == r + window(j))
        r, c = iota((D, REST), 0), iota((D, REST), 1)
        pick_rest[...] = one_hot(source_rest(c) == r)

    for part in range(3):
        base = part * D
        for j in range(4):
            lo = base + window(j)
            qkv_o[:, MAIN_AT[part] + 256 * j : MAIN_AT[part] + 256 * (j + 1)] = dot(
                qkv_ref[:, lo : lo + 384], pick[j]
            ).astype(BF16)
        qkv_o[:, REST_AT[part] : REST_AT[part] + REST] = dot(
            qkv_ref[:, base : base + D], pick_rest[...]
        ).astype(BF16)

    for j in range(4):
        out_o[256 * j : 256 * (j + 1), :] = dot(
            pick[j], out_ref[window(j) : window(j) + 384, :], TN
        ).astype(BF16)
    out_o[MAIN:, :] = dot(pick_rest[...], out_ref[...], TN).astype(BF16)


def split_weights(w_qkv, w_out):
    steps = 3
    part = D // steps
    return pl.pallas_call(
        split_weights_kernel,
        grid=(steps,),
        in_specs=[
            pl.BlockSpec((part, 3 * D), lambda i: (i, 0)),
            pl.BlockSpec((D, part), lambda i: (0, i)),
        ],
        out_specs=[
            pl.BlockSpec((part, 3 * D), lambda i: (i, 0)),
            pl.BlockSpec((D, part), lambda i: (0, i)),
        ],
        out_shape=[
            jax.ShapeDtypeStruct((D, 3 * D), BF16),
            jax.ShapeDtypeStruct((D, D), BF16),
        ],
        scratch_shapes=[pltpu.VMEM((4, 384, 256), BF16), pltpu.VMEM((D, REST), BF16)],
        compiler_params=pltpu.CompilerParams(vmem_limit_bytes=60 * MIB),
        cost_estimate=pl.CostEstimate(
            flops=2 * D * D * 1600, bytes_accessed=16 * D * D, transcendentals=0
        ),
        name="split_weights",
    )(w_qkv, w_out)


def trade(first, second, chunk):
    upper = iota(first.shape, 1) < POS
    if chunk == 0:
        return jnp.where(upper, first, pltpu.roll(second, POS, 1))
    return jnp.where(upper, pltpu.roll(first, POS, 1), second)


def pack_kernel(chunk, lat_ref, cot_ref, *refs):
    o_ref = refs[-1]
    ranks, _, width = o_ref.shape
    for c in range(TILES):
        cols = slice(LANES * c, LANES * (c + 1))
        halves = []
        for ref in (lat_ref, cot_ref):
            tiles = [ref[0, i, :, cols].astype(F32).reshape(ranks, 8, LANES) for i in range(2)]
            halves.append(trade(*tiles, chunk))
        o_ref[:, :, cols] = jnp.concatenate(halves, 1).astype(BF16)


def pack(latents, cotangent, chunk, after=()):
    _, frames, positions, width = latents.shape
    steps = 2
    ranks = positions // 8
    spec = pl.BlockSpec((1, frames, positions // steps, width), lambda i: (0, 0, i, 0))
    return pl.pallas_call(
        functools.partial(pack_kernel, chunk),
        grid=(steps,),
        in_specs=[spec, spec] + [pl.BlockSpec(memory_space=pl.ANY)] * len(after),
        out_specs=pl.BlockSpec((ranks // steps, ROWS_IN, width), lambda i: (i, 0, 0)),
        out_shape=jax.ShapeDtypeStruct((ranks, ROWS_IN, width), BF16),
        compiler_params=pltpu.CompilerParams(vmem_limit_bytes=60 * MIB),
        cost_estimate=pl.CostEstimate(flops=4_000_000, bytes_accessed=3_600_000, transcendentals=0),
        name="pack",
    )(latents, cotangent, *after)


def tie_kernel(value_ref, other_ref, o_ref):
    del value_ref, other_ref, o_ref


def tie(value, other):
    any_space = pl.BlockSpec(memory_space=pl.ANY)
    return pl.pallas_call(
        tie_kernel,
        in_specs=[any_space, any_space],
        out_specs=any_space,
        out_shape=jax.ShapeDtypeStruct(value.shape, value.dtype),
        input_output_aliases={0: 0},
        compiler_params=pltpu.CompilerParams(vmem_limit_bytes=MIB),
        name="tie",
    )(value, other)


def unpack_kernel(first_ref, second_ref, block_ref, grad_ref):
    ranks = first_ref.shape[0]
    for c in range(TILES):
        cols = slice(LANES * c, LANES * (c + 1))
        first, second = first_ref[:, :, cols].astype(F32), second_ref[:, :, cols].astype(F32)
        for at, ref in ((0, block_ref), (8, grad_ref)):
            for i in range(2):
                tile = trade(first[:, at : at + 8], second[:, at : at + 8], i)
                ref[0, i, :, cols] = tile.reshape(ranks * 8, LANES).astype(BF16)


def unpack(first, second, shape):
    _, frames, positions, width = shape
    steps = 2
    spec = pl.BlockSpec((1, frames, positions // steps, width), lambda i: (0, 0, i, 0))
    out = jax.ShapeDtypeStruct(shape, BF16)
    return pl.pallas_call(
        unpack_kernel,
        grid=(steps,),
        in_specs=[
            pl.BlockSpec((x.shape[0] // steps, ROWS_IN, width), lambda i: (i, 0, 0))
            for x in (first, second)
        ],
        out_specs=[spec, spec],
        out_shape=[out, out],
        compiler_params=pltpu.CompilerParams(vmem_limit_bytes=50 * MIB),
        cost_estimate=pl.CostEstimate(flops=4_000_000, bytes_accessed=5_000_000, transcendentals=0),
        name="unpack",
    )(first, second)


def init_segments(seg, spread, fold):
    r, c = iota((D, REST), 0), iota((D, REST), 1)
    head = jnp.where(r < MAIN, r >> 6, (r - MAIN) >> 3)
    seg[...] = one_hot(head == (c >> 3))
    entry = jnp.where(r < MAIN, r & 63, 64 + (r & 7))
    fold[...] = one_hot(entry == c)
    r, c = iota((2 * REST, MAIN), 0), iota((2 * REST, MAIN), 1)
    spread[...] = one_hot((r & (REST - 1)) == 8 * (c >> 6))


def terms(value):
    high = value.astype(BF16)
    left = value - high.astype(F32)
    mid = left.astype(BF16)
    return high, mid, (left - mid.astype(F32)).astype(BF16)


def both(per_head):
    high = per_head.astype(BF16)
    return jnp.concatenate([high, (per_head - high.astype(F32)).astype(BF16)], 1)


def head_masks(t):
    c = iota((1, 256), 1)
    head = jnp.where(c < 128, (c >> 6) + 2 * t, (c - 128) >> 3)
    return [one_hot(head == h) for h in (2 * t, 2 * t + 1)]


def unit_of(ref, rows, t):
    return jnp.concatenate([ref[rows, 128 * t : 128 * (t + 1)], ref[rows, MAIN:]], 1)


def stacked(block, masks):
    return [
        jnp.concatenate([block[:FR] * masks[0], block[:FR] * masks[1]], 0),
        jnp.concatenate([block[FR:] * masks[0], block[FR:] * masks[1]], 0),
    ]


def diagonal(block):
    zero = jnp.zeros((FR, 256), BF16)
    return jnp.concatenate(
        [
            jnp.concatenate([block[:FR], zero], 1),
            jnp.concatenate([zero, block[FR:]], 1),
        ],
        0,
    )


def by_position(block):
    lane, zero = iota((128, 128), 1), jnp.zeros((128, 128), F32)
    own = lane < FR
    return jnp.concatenate(
        [jnp.where(own, block, zero), jnp.where(own, zero, block)], 0
    ).astype(BF16)


def own_rows(product, masks):
    zero, one = masks[0].astype(F32), masks[1].astype(F32)
    return jnp.concatenate(
        [
            product[:64] * zero + product[64:128] * one,
            product[128:192] * zero + product[192:] * one,
        ],
        0,
    )


def loop(count, body):
    def step(i, _):
        body(i)
        return 0

    lax.fori_loop(0, count, step, 0)


def over_columns(total, body):
    for b in range(0, total, BLOCK):
        body(slice(b, min(b + BLOCK, total)))


def over_rows(size, body):
    for i in range(0, TOK, size):
        body(slice(i, i + size))


def lane_tiles():
    return [slice(LANES * c, LANES * (c + 1)) for c in range(TILES)]


def sub_block(
    last,
    count_ref,
    in_hbm,
    table_hbm,
    clip_hbm,
    q_gain_hbm,
    k_gain_hbm,
    wqkv_hbm,
    wout_hbm,
    before_hbm,
    out_ref,
    sums,
    table_ref,
    clip_ref,
    q_gain_ref,
    k_gain_ref,
    before_ref,
    in_ref,
    wqkv,
    wout,
    sems,
    frames,
    xp,
    unit,
    istd,
    cp,
    gy,
    normed,
    proj,
    gatt,
    qn,
    kn,
    vn,
    rq,
    rk,
    dq,
    dk,
    dqkv,
    seg,
    spread,
    fold,
    bias,
    mod_ref,
    gain_ref,
):
    ranks = in_ref.shape[0]
    used = ranks * ROWS_IN
    att, gn = gy, normed
    load_qkv = pltpu.make_async_copy(wqkv_hbm, wqkv, sems.at[0])
    load_out = pltpu.make_async_copy(wout_hbm, wout, sems.at[1])
    load_in = pltpu.make_async_copy(in_hbm, in_ref, sems.at[2])
    small = [
        pltpu.make_async_copy(source, target, sems.at[3 + i])
        for i, (source, target) in enumerate(
            (
                (table_hbm, table_ref),
                (clip_hbm, clip_ref),
                (q_gain_hbm, q_gain_ref),
                (k_gain_hbm, k_gain_ref),
                (before_hbm, before_ref),
            )
        )
    ]
    load_in.start()
    for copy in small:
        copy.start()
    load_out.start()
    load_qkv.start()
    init_segments(seg, spread, fold)
    key = iota((128, 128), 0) & (FR - 1)
    valid = 2 * (key & 31) + (key >> 5) < count_ref[0]
    bias[...] = jnp.where(valid, jnp.float32(0), jnp.float32(-1e30))
    for copy in small:
        copy.wait()
    sums[...] = before_ref[...]
    mod_ref[...] = table_ref[...] + clip_ref[...]
    for part, ref in enumerate((q_gain_ref, k_gain_ref)):
        gain_ref[part : part + 1, :] = sum(dot(x, fold[:, :HEAD], NT) for x in terms(ref[...]))

    def strided(p, first, own):
        return pl.ds(first + own * POS + p, ranks, stride=ROWS_IN)

    def gather(c, p, first):
        return jnp.concatenate([frames[c, strided(p, first, own), :] for own in range(2)], 0)

    def scatter(c, p, first, value):
        for own in range(2):
            frames[c, strided(p, first, own), :] = value[own * ranks : (own + 1) * ranks]

    def position_rows(p):
        if isinstance(p, int):
            return slice(p * FR, (p + 1) * FR)
        return pl.ds(pl.multiple_of(p * FR, FR), FR)

    load_in.wait()
    for c, cols in enumerate(lane_tiles()):
        frames[c, :used] = in_ref[:, :, cols].reshape(used, LANES).astype(F32)

    def arrive(p):
        rows = position_rows(p)
        for c, cols in enumerate(lane_tiles()):
            cot = gather(c, p, 8)
            cp[rows, cols] = cot
            gy[rows, cols] = (cot * mod_ref[2:3, cols]).astype(BF16)

    def norm(p):
        rows = position_rows(p)
        parts = [gather(c, p, 0) for c in range(TILES)]
        mean = jnp.sum(sum(parts), -1, keepdims=True) * (1.0 / D)
        centred = [x - mean for x in parts]
        square = jnp.sum(sum(x * x for x in centred), -1, keepdims=True) * (1.0 / D)
        inv = lax.rsqrt(square + EPS)
        istd[rows, :] = jnp.broadcast_to(inv, (FR, LANES))
        for c, cols in enumerate(lane_tiles()):
            xp[rows, cols] = parts[c]
            u = centred[c] * inv
            unit[rows, cols] = u
            normed[rows, cols] = (u * (1.0 + mod_ref[1:2, cols]) + mod_ref[0:1, cols]).astype(BF16)

    loop(POS, arrive)

    def grad_attention(cols):
        gatt[:, cols] = dot(gy[...], wout[cols, :], NT).astype(BF16)

    load_out.wait()
    norm(0)
    grad_attention(slice(0, BLOCK))
    norm(1)
    grad_attention(slice(BLOCK, 2 * BLOCK))
    norm(2)
    grad_attention(slice(2 * BLOCK, D))
    norm(3)

    def project(cols):
        proj[:, cols] = dot(normed[...], wqkv[:, cols])

    load_qkv.wait()
    over_columns(QK, project)

    def project_values(cols):
        vn[:, cols] = dot(normed[...], wqkv[:, QK + cols.start : QK + cols.stop]).astype(BF16)


    def heads(part, n_ref, r_ref, rows):
        main = slice(MAIN_AT[part], MAIN_AT[part] + MAIN)
        rest = slice(REST_AT[part], REST_AT[part] + REST)
        m, t = proj[rows, main], proj[rows, rest]
        total = sum(dot(part, seg[:MAIN, :]) for part in terms(m * m)[:2])
        total = total + sum(dot(part, seg[MAIN:, :]) for part in terms(t * t)[:2])
        inv = lax.rsqrt(total * (1.0 / HEAD) + EPS)
        r_ref[rows, :] = inv
        pair = both(inv)
        for b in range(0, MAIN, 256):
            cols = slice(MAIN_AT[part] + b, MAIN_AT[part] + b + 256)
            hat = proj[rows, cols] * dot(pair, spread[:, b : b + 256])
            proj[rows, cols] = hat
            n_ref[rows, b : b + 256] = (hat * gain_ref[part : part + 1, b : b + 256]).astype(BF16)
        hat = t * inv
        proj[rows, rest] = hat
        n_ref[rows, MAIN:] = (hat * gain_ref[part : part + 1, MAIN:]).astype(BF16)


    everything = slice(0, TOK)
    project_values(slice(0, BLOCK))
    heads(0, qn, rq, everything)
    project_values(slice(BLOCK, 2 * BLOCK))
    heads(1, kn, rk, everything)
    project_values(slice(2 * BLOCK, D))

    def attend(rows):
        rest = [jnp.zeros((ROWS, REST), F32)] * 4
        ops, soft = [], []
        for t in range(HEADS // 2):
            masks = head_masks(t)
            keys = stacked(unit_of(kn, rows, t), masks)
            vals = stacked(unit_of(vn, rows, t), masks)
            query = diagonal(unit_of(qn, rows, t))
            grad = diagonal(unit_of(gatt, rows, t))
            s = dot(jnp.concatenate(keys, 1), query, NT) * (HEAD**-0.5) + bias[...]
            dp = dot(jnp.concatenate(vals, 1), grad, NT)
            ops.append((t, masks, keys, vals, s, dp))
        for *_, s, dp in ops:
            s, dp = s.reshape(2, FR, 128), dp.reshape(2, FR, 128)
            e = jnp.exp(s - jnp.max(s, 1, keepdims=True))
            prob = e * (1.0 / jnp.sum(e, 1, keepdims=True))
            delta = jnp.sum(prob * dp, 1, keepdims=True)
            ds = (prob * (dp - delta) * (HEAD**-0.5)).reshape(128, 128)
            prob = prob.reshape(128, 128)
            soft.append((prob, ds))
        for (t, masks, keys, vals, _, _), (prob, ds) in zip(ops, soft):
            pt, dt = prob.T.astype(BF16), ds.T.astype(BF16)
            cols = slice(128 * t, 128 * (t + 1))
            out = jnp.concatenate([dot(pt[:FR], vals[0]), dot(pt[FR:], vals[1])], 0)
            gq = jnp.concatenate([dot(dt[:FR], keys[0]), dot(dt[FR:], keys[1])], 0)
            gk = own_rows(dot(by_position(ds), unit_of(qn, rows, t)), masks)
            gv = own_rows(dot(by_position(prob), unit_of(gatt, rows, t)), masks)
            att[rows, cols] = out[:, :128].astype(BF16)
            dq[rows, cols] = gq[:, :128].astype(BF16)
            dk[rows, cols] = gk[:, :128].astype(BF16)
            dqkv[rows, QK + 128 * t : QK + 128 * (t + 1)] = gv[:, :128].astype(BF16)
            rest = [a + b[:, 128:] for a, b in zip(rest, (out, gq, gk, gv))]
        att[rows, MAIN:] = rest[0].astype(BF16)
        dq[rows, MAIN:] = rest[1].astype(BF16)
        dk[rows, MAIN:] = rest[2].astype(BF16)
        dqkv[rows, QK + MAIN :] = rest[3].astype(BF16)

    over_rows(ROWS, attend)

    def out_project(first, size):
        cols = slice(first, first + size)
        y = dot(att[...], wout[:, cols])
        sums[2:3, cols] += jnp.sum(cp[:, cols] * y, 0, keepdims=True)
        value = xp[:, cols] + mod_ref[2:3, cols] * y
        for c in range(size // LANES):
            for p in range(POS):
                tile = value[p * FR : (p + 1) * FR, c * LANES : (c + 1) * LANES]
                scatter(first // LANES + c, p, 0, tile)


    def heads_grad(part, d_ref, r_ref, rows):
        main = slice(MAIN_AT[part], MAIN_AT[part] + MAIN)
        rest = slice(REST_AT[part], REST_AT[part] + REST)
        gain = gain_ref[part : part + 1, :]
        row = slice(3 + part, 4 + part)
        um, ur = d_ref[rows, :MAIN].astype(F32), d_ref[rows, MAIN:].astype(F32)
        wm, wr = um * proj[rows, main], ur * proj[rows, rest]
        sums[row, :MAIN] += jnp.sum(wm, 0, keepdims=True)
        sums[row, MAIN:] += jnp.sum(wr, 0, keepdims=True)
        total = dot((wm * gain[:, :MAIN]).astype(BF16), seg[:MAIN, :]) + dot(
            (wr * gain[:, MAIN:]).astype(BF16), seg[MAIN:, :]
        )
        inner = total * (1.0 / HEAD)
        inv = r_ref[rows, :]
        pair, inner_pair = both(inv), both(inner)
        for b in range(0, MAIN, 256):
            cols = slice(MAIN_AT[part] + b, MAIN_AT[part] + b + 256)
            a = d_ref[rows, b : b + 256].astype(F32) * gain[:, b : b + 256]
            picked = spread[:, b : b + 256]
            value = dot(pair, picked) * (a - proj[rows, cols] * dot(inner_pair, picked))
            dqkv[rows, cols] = value.astype(BF16)
        value = inv * (ur * gain[:, MAIN:] - proj[rows, rest] * inner)
        dqkv[rows, rest] = value.astype(BF16)


    out_project(0, BLOCK)
    heads_grad(0, dq, rq, everything)
    out_project(BLOCK, BLOCK)
    heads_grad(1, dk, rk, everything)
    out_project(2 * BLOCK, D - 2 * BLOCK)

    def grad_normed(cols):
        gn[:, cols] = dot(dqkv[...], wqkv[cols, :], NT).astype(BF16)

    over_columns(D, grad_normed)

    def layer(p):
        rows = position_rows(p)
        grads = [gn[rows, cols].astype(F32) for cols in lane_tiles()]
        units = [unit[rows, cols] for cols in lane_tiles()]
        scaled = []
        for g, u, cols in zip(grads, units, lane_tiles()):
            sums[0:1, cols] += jnp.sum(g, 0, keepdims=True)
            sums[1:2, cols] += jnp.sum(g * u, 0, keepdims=True)
            scaled.append(g * (1.0 + mod_ref[1:2, cols]))
        first = jnp.sum(sum(scaled), -1, keepdims=True) * (1.0 / D)
        second = jnp.sum(sum(g * u for g, u in zip(scaled, units)), -1, keepdims=True) * (1.0 / D)
        inv = istd[rows, :]
        for c, cols in enumerate(lane_tiles()):
            value = cp[rows, cols] + inv * (scaled[c] - first - units[c] * second)
            scatter(c, p, 8, value)

    for p in range(POS):
        layer(p)

    if last:
        total = sums[...]
        folded = sum(dot(part, fold[...]) for part in terms(total))
        gains = jnp.concatenate([folded[3:4], folded[4:5], jnp.zeros((1, D - 256), F32)], 1)
        high, low, _ = terms(jnp.concatenate([total[:3], gains], 0))
        sent = jnp.concatenate([high.astype(F32), low.astype(F32)], 0)
    for c, cols in enumerate(lane_tiles()):
        block = frames[c, :used].reshape(ranks, ROWS_IN, LANES)
        if last:
            rows = jnp.broadcast_to(sent[None, :, cols], (ranks, SUMS, LANES))
            block = jnp.concatenate([block, rows], 1)
        out_ref[:, :, cols] = block.astype(BF16)


def run_sub_block(last, frame_counts, arrived, modulation, gains, weights, before):
    ranks = arrived.shape[0]
    tok = (TOK, D)
    any_space = pl.BlockSpec(memory_space=pl.ANY)
    vmem = pl.BlockSpec(memory_space=pltpu.VMEM)
    sent = ROWS_IN + SUMS if last else ROWS_IN
    scratch = [
        pltpu.VMEM((3, D), F32),
        pltpu.VMEM((3, D), F32),
        pltpu.VMEM((1, HEAD), F32),
        pltpu.VMEM((1, HEAD), F32),
        pltpu.VMEM((8, D), F32),
        pltpu.VMEM((ranks, ROWS_IN, D), BF16),
        pltpu.VMEM((D, 3 * D), BF16),
        pltpu.VMEM((D, D), BF16),
        pltpu.SemaphoreType.DMA((8,)),
        pltpu.VMEM((TILES, (ranks + 1) * ROWS_IN, LANES), F32),
        pltpu.VMEM(tok, F32),
        pltpu.VMEM(tok, F32),
        pltpu.VMEM((TOK, LANES), F32),
        pltpu.VMEM(tok, F32),
        pltpu.VMEM(tok, BF16),
        pltpu.VMEM(tok, BF16),
        pltpu.VMEM((TOK, QK), F32),
        pltpu.VMEM(tok, BF16),
        pltpu.VMEM(tok, BF16),
        pltpu.VMEM(tok, BF16),
        pltpu.VMEM(tok, BF16),
        pltpu.VMEM((TOK, REST), F32),
        pltpu.VMEM((TOK, REST), F32),
        pltpu.VMEM(tok, BF16),
        pltpu.VMEM(tok, BF16),
        pltpu.VMEM((TOK, 3 * D), BF16),
        pltpu.VMEM((D, REST), BF16),
        pltpu.VMEM((2 * REST, MAIN), BF16),
        pltpu.VMEM((D, REST), BF16),
        pltpu.VMEM((128, 128), F32),
        pltpu.VMEM((3, D), F32),
        pltpu.VMEM((2, D), F32),
    ]
    return pl.pallas_call(
        functools.partial(sub_block, last),
        in_specs=[pl.BlockSpec(memory_space=pltpu.SMEM)]
        + [any_space] * 8,
        out_specs=[vmem, vmem],
        out_shape=[
            jax.ShapeDtypeStruct((ranks, sent, D), BF16),
            jax.ShapeDtypeStruct((8, D), F32),
        ],
        scratch_shapes=scratch,
        compiler_params=pltpu.CompilerParams(vmem_limit_bytes=50 * MIB),
        cost_estimate=pl.CostEstimate(
            flops=12_000_000_000, bytes_accessed=20_000_000, transcendentals=0
        ),
        name="sub_block",
    )(frame_counts, arrived, *modulation, *gains, *weights, before)


def sum_clips(value):
    clips = lax.axis_size("dp")
    one, two, three = (
        lax.ppermute(value, "dp", [(i, i ^ step) for i in range(clips)]) for step in (1, 2, 3)
    )
    return (value + one) + (two + three)


def shards(latents, frame_counts, mod_table, clip_mod, q_gain, k_gain, w_qkv, w_out, cotangent):
    ranks = lax.axis_size("seq")
    modulation = (mod_table, clip_mod[0])
    gains = (q_gain[None], k_gain[None])

    def exchange(rows):
        return lax.all_to_all(rows, "seq", split_axis=0, concat_axis=0, tiled=True)

    weights = split_weights(w_qkv, w_out)
    arrived = [
        exchange(pack(latents, cotangent, 0)),
        exchange(pack(latents, cotangent, 1, after=weights[1:])),
    ]
    sums = jnp.zeros((8, D), F32)
    back = []
    for i in range(CHUNKS):
        last = i == CHUNKS - 1
        out, sums = run_sub_block(last, frame_counts, arrived[i], modulation, gains, weights, sums)
        back.append(exchange(tie(out, back[0]) if last else out))
    pieces = jnp.sum(back[-1][:, ROWS_IN:, :].astype(F32), 0)
    clip_total = pieces[0:4] + pieces[4:8]
    total = sum_clips(clip_total)
    block_out, input_grad = unpack(*back, latents.shape)
    return (
        block_out,
        input_grad,
        clip_total[None, :3],
        total[:3],
        total[3, :HEAD],
        total[3, 128 : 128 + HEAD],
    )


def solution(mesh):
    return jax.shard_map(
        shards,
        mesh=mesh,
        in_specs=(
            P("dp", "seq", None, None),
            P("dp"),
            P(),
            P("dp", None, None),
            P(),
            P(),
            P(),
            P(),
            P("dp", "seq", None, None),
        ),
        out_specs=(
            P("dp", "seq", None, None),
            P("dp", "seq", None, None),
            P("dp", None, None),
            P(),
            P(),
            P(),
        ),
        check_vma=False,
    )
```
